32 devices in a mesh: group: 4 (over y, x), expert: 8 (over z, core).
Axes of the slice: x: 2, y: 2, z: 4, core: 2. Of those that a mesh axis runs over, the one named last changes fastest.
Arguments:
- tokens: bfloat16 [128, 7168], P(('group', 'expert')), may hold values from -6 to 6
- expert_ids: int32 [128, 8], P(('group', 'expert')), may hold values from 0 to 31, all different within a row; in each aligned block of 4 rows (0 to 3, 4 to 7, ...) at most 2 rows name the same one
- gate_weights: bfloat16 [128, 8], P(('group', 'expert')), may hold values from 0.049804688 to 0.5
- w_gate: bfloat16 [32, 7168, 2048], P(('group', 'expert')), may hold values from -0.0625 to 0.0625
- w_up: bfloat16 [32, 7168, 2048], P(('group', 'expert')), may hold values from -0.0625 to 0.0625
- w_down: bfloat16 [32, 2048, 7168], P(('group', 'expert')), may hold values from -0.125 to 0.125
Outputs:
- mixed: bfloat16 [128, 7168], P(('group', 'expert'))
The draws below stay inside these ranges and needn't reach their ends.
Inputs may be any that keep to these rules, and one draw needn't show every extreme that they name: `expert_ids`: each row names 8 different experts. Among the 4 rows of one device no expert is named by more than 2 rows, and in some device some expert is named by exactly 2 rows.
All inputs are finite; a program needn't handle non-finite values.
Results may differ from the reference program's by a relative error of at most 0.014.
Values may be sent and summed in bfloat16 or wider, within the bound.
No kernel may reach another device: no remote copies, remote signals or barrier semaphores. Data moves between devices by JAX's collectives and lax.ppermute only.
A program may use at most 128 MiB of HBM per device.

```python
import math
import jax
import jax.numpy as jnp
import numpy as np
from jax import lax

D = 7168
FF = 2048
TOP = 8
EXP_GRP = 8
ROWS = 4
CAP = 2
EXPERTS = 32
SPLIT = 1
FF_SHARD = 2048
TOKENS = 128
N_GROUP = 4
N_EXPERT = 8


def block_scale(rng, dims, cuts, least, largest):
    def one(position, blocks):
        heights = jax.random.uniform(jax.random.fold_in(jax.random.fold_in(rng, 6), position), (blocks,), jnp.float32, least / len(cuts), largest / len(cuts))
        return jnp.repeat(jnp.exp(heights), dims[position] // blocks).reshape((-1,) + (1,) * (len(dims) - position - 1))

    factor_of = one(*cuts[0])
    for cut in cuts[1:]:
        factor_of = factor_of * one(*cut)
    return factor_of


def shared_out(own_key, own, number, rows, amount, top, reach, slope):
    sequence = jax.random.permutation(own_key, amount)
    heavy_load, ordinary = load_shares(amount, rows * top, reach, slope, True), load_shares(amount, rows * top, reach, slope, False)
    places = jnp.arange(amount)

    def named(tallies, offset_by):
        used = int((tallies > 0).sum())
        fixed = max(1, used // 4)
        moved = fixed + (places - fixed + offset_by * (used - fixed)) % max(1, amount - fixed)
        return jnp.zeros((amount,), jnp.int32).at[sequence[jnp.where(places < fixed, places, moved)]].set(jnp.asarray(tallies, jnp.int32))

    tallies = jnp.where(number % 4 == 0, named(heavy_load, number // 4), named(ordinary, number - number // 4 - 1))
    mixed = jax.random.permutation(jax.random.fold_in(own, 3), amount)
    giver, sink = mixed[0:amount // 2 * 2:2], mixed[1:amount // 2 * 2:2]
    room = jnp.minimum(tallies[giver] - 1, reach - tallies[sink]) // 2
    room = jnp.where((giver == sequence[0]) | (sink == sequence[0]) | (tallies[sink] == 0), 0, jnp.maximum(room, 0))
    moved = jax.random.randint(jax.random.fold_in(own, 4), (amount // 2,), 0, 1 << 20) % (room + 1)
    tallies = tallies.at[giver].add(-moved).at[sink].add(moved)
    items = jnp.searchsorted(jnp.cumsum(tallies), jnp.arange(rows * top), side="right").astype(jnp.int32)
    grid = items.reshape(top, rows).T
    grid = grid[jax.random.permutation(jax.random.fold_in(own, 1), rows)]
    offset_by = jax.random.randint(jax.random.fold_in(own, 2), (rows, 1), 0, top)
    return jnp.take_along_axis(grid, (jnp.arange(top)[None, :] + offset_by) % top, axis=1)


def load_shares(amount, total, reach, slope, full):
    loads = [(1 << 20) // math.isqrt(rank ** slope) + 1 for rank in range(1, amount + 1)]
    largest = reach if full else min(reach, max(-(-total // amount), total * loads[0] // sum(loads)))
    least = 1 if total - largest >= amount - 1 else 0
    counts, spare = [largest] + [least] * (amount - 1), total - largest - least * (amount - 1)
    while spare > 0:
        free = [i for i in range(1, amount) if counts[i] < largest] or [i for i in range(1, amount) if counts[i] < reach]
        pool, budget = sum([loads[i] for i in free]), spare
        for i in free:
            extra = min(reach - counts[i], max(1, budget * loads[i] // pool), spare)
            counts[i] = counts[i] + extra
            spare = spare - extra
    return np.array(counts)


def centred(key, dims, spread, bound, cuts=(), held_as=jnp.bfloat16):
    result = spread * jax.random.normal(key, dims, jnp.float32)
    if cuts:
        result = result * block_scale(key, dims, cuts, -0.22, 0.18)
    return jnp.clip(result, -bound, bound).astype(held_as)


def setup_inputs(seed: int = 0) -> dict:
    key_of = jax.random.split(jax.random.key(seed), 7)
    tokens = centred(key_of[0], (TOKENS, D), 1.0, 6.0, ((0, 32),))
    expert_ids_keys = jax.random.split(jax.random.fold_in(key_of[1], 1), TOKENS // ROWS)
    expert_ids_turns = jax.random.permutation(jax.random.fold_in(key_of[1], 3), TOKENS // ROWS)
    expert_ids = jax.vmap(lambda own, number: shared_out(jax.random.fold_in(key_of[1], 2), own, number, ROWS, EXPERTS, TOP, CAP, 2))(expert_ids_keys, expert_ids_turns).reshape((TOKENS, TOP))
    gate_weights = jnp.clip(jnp.exp(math.log(0.5) - 2.306499 * jax.random.uniform(key_of[2], (TOKENS, TOP), jnp.float32) ** block_scale(key_of[2], (TOKENS, TOP), ((0, 32),), -0.2, 0.2)), 0.049804688, 0.5).astype(jnp.bfloat16)
    w_gate = centred(key_of[3], (EXPERTS * SPLIT, D, FF_SHARD), D ** -0.5, 0.0625, ((0, 32),))
    w_up = centred(key_of[4], (EXPERTS * SPLIT, D, FF_SHARD), D ** -0.5, 0.0625, ((0, 32),))
    w_down = centred(key_of[5], (EXPERTS * SPLIT, FF_SHARD, D), FF ** -0.5, 0.125, ((0, 32),))
    return {"tokens": tokens, "expert_ids": expert_ids, "gate_weights": gate_weights, "w_gate": w_gate, "w_up": w_up, "w_down": w_down}


def reference(tokens, expert_ids, gate_weights, w_gate, w_up, w_down):
    experts = N_GROUP * EXP_GRP
    split = N_EXPERT // EXP_GRP
    total = tokens.shape[0]
    width = tokens.shape[1]
    labels = jnp.arange(experts, dtype=jnp.int32)
    match = expert_ids[:, :, None] == labels[None, None, :]
    named = jnp.any(match, axis=1)
    weight = jnp.sum(jnp.where(match, gate_weights.astype(jnp.float32)[:, :, None], jnp.float32(0.0)), axis=1)
    most = N_GROUP * N_EXPERT * CAP

    def one_expert(carry, index):
        column = named[:, index]
        picked = jnp.nonzero(column, size=most, fill_value=0)[0].astype(jnp.int32)
        valid = jnp.arange(most, dtype=jnp.int32) < jnp.sum(column.astype(jnp.int32))
        rows = tokens[picked]
        start = (index * split).astype(jnp.int32)
        gate_rows = lax.dynamic_slice_in_dim(w_gate, start, split, 0)
        up_rows = lax.dynamic_slice_in_dim(w_up, start, split, 0)
        down_rows = lax.dynamic_slice_in_dim(w_down, start, split, 0)
        gate_full = jnp.transpose(gate_rows, (1, 0, 2)).reshape(width, -1)
        up_full = jnp.transpose(up_rows, (1, 0, 2)).reshape(width, -1)
        gate_val = jnp.dot(rows, gate_full, preferred_element_type=jnp.float32)
        up_val = jnp.dot(rows, up_full, preferred_element_type=jnp.float32)
        hidden = (jax.nn.silu(gate_val) * up_val).astype(jnp.bfloat16)
        hidden = hidden.reshape(most, split, -1)
        parts = jnp.einsum("msf,sfd->msd", hidden.astype(jnp.float32), down_rows.astype(jnp.float32),
                           precision=lax.Precision.HIGHEST).astype(jnp.bfloat16)
        expert_out = jnp.sum(parts.astype(jnp.float32), axis=1).astype(jnp.bfloat16)
        scale = jnp.where(valid, weight[picked, index], jnp.float32(0.0))
        carry = carry.at[picked].add(scale[:, None] * expert_out.astype(jnp.float32))
        return carry, None

    summed, _ = lax.scan(one_expert, jnp.zeros((total, width), jnp.float32), labels)
    return summed.astype(jnp.bfloat16)
```

```python
import jax
import jax.numpy as jnp
from jax import lax
from jax.sharding import PartitionSpec as P

EXP_GRP = 8
AXES = ("group", "expert")


def on_device(tokens, expert_ids, gate_weights, w_gate, w_up, w_down):
    groups = lax.axis_size("group")
    members = lax.axis_size("expert")
    split = members // EXP_GRP
    experts = groups * EXP_GRP
    width = tokens.shape[1]
    me = lax.axis_index("group") * EXP_GRP + lax.axis_index("expert") // split
    labels = jnp.arange(experts, dtype=jnp.int32)
    match = expert_ids[:, :, None] == labels[None, None, :]
    weight = jnp.sum(
        jnp.where(match, gate_weights.astype(jnp.float32)[:, :, None], jnp.float32(0.0)), axis=1
    ).astype(jnp.bfloat16)
    pad = -(-experts // 128) * 128 - experts
    packed = jnp.concatenate([tokens, jnp.pad(weight, ((0, 0), (0, pad)))], axis=1)
    everyone = lax.all_gather(packed, AXES, axis=0, tiled=True)
    rows = everyone[:, :width]
    mine = labels == me
    scale = jnp.sum(
        jnp.where(mine[None, :], everyone[:, width : width + experts].astype(jnp.float32), 0.0),
        axis=1,
        keepdims=True,
    )
    gate_val = jnp.dot(rows, w_gate[0], preferred_element_type=jnp.float32)
    up_val = jnp.dot(rows, w_up[0], preferred_element_type=jnp.float32)
    hidden = (jax.nn.silu(gate_val) * up_val).astype(jnp.bfloat16)
    part = jnp.dot(hidden, w_down[0], preferred_element_type=jnp.float32)
    part = (part * scale).astype(jnp.bfloat16)
    return lax.psum_scatter(part, AXES, scatter_dimension=0, tiled=True)


def solution(mesh):
    in_specs = (
        P(AXES, None),
        P(AXES, None),
        P(AXES, None),
        P(AXES, None, None),
        P(AXES, None, None),
        P(AXES, None, None),
    )
    out_specs = P(AXES, None)
    return jax.shard_map(
        on_device, mesh=mesh, in_specs=in_specs, out_specs=out_specs, check_vma=False
    )
```

```python
import functools

import jax
import jax.numpy as jnp
from jax import lax
from jax.experimental import pallas as pl
from jax.experimental.pallas import tpu as pltpu
from jax.sharding import PartitionSpec as P

EXP_GRP = 8
AXES = ("group", "expert")
CHUNKS = 2
LIMIT = 24 * 1024 * 1024


def block_of(total, most):
    size = most
    while total % size:
        size -= 128
    return size


def shifted(value, axis, size, shift, unit=1):
    count = size // unit
    pairs = []
    for i in range(size):
        slot, low = i // unit, i % unit
        pairs.append((i, ((slot + shift) % count) * unit + low))
    return lax.ppermute(value, axis, pairs)


def other_core(value, size):
    return lax.ppermute(value, "expert", [(i, i ^ 1) for i in range(size)])


def gather(value, groups, members):
    lines = members // 2
    column = jnp.concatenate(
        [value] + [shifted(value, "expert", members, s, 2) for s in range(1, lines)], axis=0
    )
    planes = [column] + [shifted(column, "group", groups, s) for s in range(1, groups)]
    return planes + [other_core(p, members) for p in planes]


def gate_up_kernel(parts, has_acc, last, *refs):
    x_refs = refs[:parts]
    gate_ref, up_ref = refs[parts : parts + 2]
    rest = refs[parts + 2 :]
    if has_acc:
        gate_in, up_in = rest[:2]
        rest = rest[2:]
    if last:
        hidden_ref, gate_acc, up_acc = rest
    else:
        gate_acc, up_acc = rest
    step = pl.program_id(0)
    x = jnp.concatenate([r[...] for r in x_refs], axis=0)
    gate = jnp.dot(x, gate_ref[0], preferred_element_type=jnp.float32)
    up = jnp.dot(x, up_ref[0], preferred_element_type=jnp.float32)

    @pl.when(step == 0)
    def _():
        if has_acc:
            gate_acc[...] = gate_in[...] + gate
            up_acc[...] = up_in[...] + up
        else:
            gate_acc[...] = gate
            up_acc[...] = up

    @pl.when(step > 0)
    def _():
        gate_acc[...] += gate
        up_acc[...] += up

    if last:

        @pl.when(step == pl.num_programs(0) - 1)
        def _():
            hidden_ref[...] = (jax.nn.silu(gate_acc[...]) * up_acc[...]).astype(jnp.bfloat16)


def gate_up(parts, w_gate, w_up, start, acc, last, width):
    rows = sum(p.shape[0] for p in parts)
    units = w_gate.shape[2]
    block = block_of(width, 512)
    first = start // block
    steps = width // block
    weight_spec = pl.BlockSpec((1, block, units), lambda i: (0, first + i, 0))
    whole = pl.BlockSpec((rows, units), lambda i: (0, 0))
    in_specs = [pl.BlockSpec((p.shape[0], block), lambda i: (0, i)) for p in parts]
    in_specs += [weight_spec, weight_spec]
    args = list(parts) + [w_gate, w_up]
    if acc is not None:
        in_specs += [whole, whole]
        args += list(acc)
    total = jax.ShapeDtypeStruct((rows, units), jnp.float32)
    if last:
        out_shape = jax.ShapeDtypeStruct((rows, units), jnp.bfloat16)
        out_specs = whole
        scratch = [pltpu.VMEM((rows, units), jnp.float32)] * 2
    else:
        out_shape = (total, total)
        out_specs = (whole, whole)
        scratch = []
    return pl.pallas_call(
        functools.partial(gate_up_kernel, len(parts), acc is not None, last),
        grid=(steps,),
        in_specs=in_specs,
        out_specs=out_specs,
        out_shape=out_shape,
        scratch_shapes=scratch,
        compiler_params=pltpu.CompilerParams(vmem_limit_bytes=LIMIT),
        cost_estimate=pl.CostEstimate(
            flops=4 * rows * width * units,
            bytes_accessed=4 * width * units,
            transcendentals=0,
        ),
    )(*args)


def down_kernel(hidden_ref, down_ref, me_ref, *refs):
    route_refs, (own_ref, far_ref) = refs[:-2], refs[-2:]
    route = jnp.concatenate([r[...] for r in route_refs], axis=0).astype(jnp.float32)
    lane = lax.broadcasted_iota(jnp.int32, route.shape, 1)
    scale = jnp.sum(jnp.where(lane == me_ref[0], route, 0.0), axis=1, keepdims=True)
    part = jnp.dot(hidden_ref[...], down_ref[0], preferred_element_type=jnp.float32)
    part = (part * scale).astype(jnp.bfloat16)
    half = part.shape[0] // 2
    own_ref[...] = part[:half]
    far_ref[...] = part[half:]


def down(hidden, w_down, routes, me, start, width):
    rows, units = hidden.shape
    block = block_of(width, 512)
    first = start // block
    half = jax.ShapeDtypeStruct((rows // 2, width), jnp.bfloat16)
    half_spec = pl.BlockSpec((rows // 2, block), lambda i: (0, i))
    return pl.pallas_call(
        down_kernel,
        grid=(width // block,),
        in_specs=[
            pl.BlockSpec((rows, units), lambda i: (0, 0)),
            pl.BlockSpec((1, units, block), lambda i: (0, 0, first + i)),
            pl.BlockSpec(memory_space=pltpu.SMEM),
        ]
        + [pl.BlockSpec(r.shape, lambda i: (0, 0)) for r in routes],
        out_specs=(half_spec, half_spec),
        out_shape=(half, half),
        compiler_params=pltpu.CompilerParams(vmem_limit_bytes=LIMIT),
        cost_estimate=pl.CostEstimate(
            flops=2 * rows * width * units,
            bytes_accessed=2 * width * units,
            transcendentals=0,
        ),
    )(hidden, w_down, me, *routes)


def add_kernel(count, *refs):
    ins, outs = refs[:count], refs[count:]
    total = ins[0][...].astype(jnp.float32)
    for ref in ins[1:]:
        total = total + ref[...].astype(jnp.float32)
    total = total.astype(jnp.bfloat16)
    size = total.shape[0] // len(outs)
    for i, ref in enumerate(outs):
        ref[...] = total[i * size : (i + 1) * size]


def add_split(values, pieces):
    rows, width = values[0].shape
    block = block_of(width, 1792)
    out = jax.ShapeDtypeStruct((rows // pieces, width), jnp.bfloat16)
    return pl.pallas_call(
        functools.partial(add_kernel, len(values)),
        grid=(width // block,),
        in_specs=[pl.BlockSpec((rows, block), lambda i: (0, i))] * len(values),
        out_specs=(pl.BlockSpec((rows // pieces, block), lambda i: (0, i)),) * pieces,
        out_shape=(out,) * pieces,
        compiler_params=pltpu.CompilerParams(vmem_limit_bytes=LIMIT),
        cost_estimate=pl.CostEstimate(
            flops=len(values) * rows * width,
            bytes_accessed=2 * (len(values) + 1) * rows * width,
            transcendentals=0,
        ),
    )(*values)


def give_back(own, far, groups, members):
    lines = members // 2
    planes = add_split([own, other_core(far, members)], groups)
    planes = [planes[0]] + [shifted(planes[s], "group", groups, -s) for s in range(1, groups)]
    column = add_split(planes, lines)
    column = [column[0]] + [
        shifted(column[s], "expert", members, -s, 2) for s in range(1, lines)
    ]
    total = column[0].astype(jnp.float32)
    for value in column[1:]:
        total = total + value.astype(jnp.float32)
    return total.astype(jnp.bfloat16)


def on_device(tokens, expert_ids, gate_weights, w_gate, w_up, w_down):
    groups = lax.axis_size("group")
    members = lax.axis_size("expert")
    split = members // EXP_GRP
    experts = groups * EXP_GRP
    width = tokens.shape[1] // CHUNKS
    me = lax.axis_index("group") * EXP_GRP + lax.axis_index("expert") // split
    labels = jnp.arange(-(-experts // 128) * 128, dtype=jnp.int32)
    match = expert_ids[:, :, None] == labels[None, None, :]
    route = jnp.sum(
        jnp.where(match, gate_weights.astype(jnp.float32)[:, :, None], jnp.float32(0.0)), axis=1
    ).astype(jnp.bfloat16)
    acc = None
    for c in range(CHUNKS):
        last = c == CHUNKS - 1
        chunk = tokens[:, c * width : (c + 1) * width]
        if last:
            chunk = jnp.concatenate([chunk, route], axis=1)
        parts = gather(chunk, groups, members)
        if last:
            routes = [p[:, width:] for p in parts]
        acc = gate_up(parts, w_gate, w_up, c * width, acc, last, width)
    hidden = acc
    me = me.astype(jnp.int32).reshape(1)
    outs = []
    for c in range(CHUNKS):
        own, far = down(hidden, w_down, routes, me, c * width, width)
        outs.append(give_back(own, far, groups, members))
    return jnp.concatenate(outs, axis=1)


def solution(mesh):
    in_specs = (
        P(AXES, None),
        P(AXES, None),
        P(AXES, None),
        P(AXES, None, None),
        P(AXES, None, None),
        P(AXES, None, None),
    )
    out_specs = P(AXES, None)
    return jax.shard_map(
        on_device, mesh=mesh, in_specs=in_specs, out_specs=out_specs, check_vma=False
    )
```

```python
import functools

import jax
import jax.numpy as jnp
from jax import lax
from jax.experimental import pallas as pl
from jax.experimental.pallas import tpu as pltpu
from jax.sharding import PartitionSpec as P

EXP_GRP = 8
CAP = 2
LANES = 128
AXES = ("group", "expert")
VMEM = pltpu.VMEM
UNIT_BLOCK = 256
DOWN_BLOCK = 512
UP_RING = 2
DOWN_RING = 3


def in_vmem(value):
    return pltpu.with_memory_space_constraint(value, VMEM)


def in_hbm(value):
    return pltpu.with_memory_space_constraint(value, pltpu.HBM)


def whole_vmem(count):
    return [pl.BlockSpec(memory_space=VMEM)] * count


def shifted(value, axis, size, shift, unit=1):
    count = size // unit
    pairs = []
    for i in range(size):
        slot, low = i // unit, i % unit
        pairs.append((i, ((slot + shift) % count) * unit + low))
    return lax.ppermute(value, axis, pairs)


def other_core(value, size):
    return lax.ppermute(value, "expert", [(i, i ^ 1) for i in range(size)])


def pack_kernel(tokens_ref, ids_ref, weights_ref, out_ref):
    width = tokens_ref.shape[1]
    out_ref[:, :width] = tokens_ref[...]
    ids = ids_ref[...]
    weights = weights_ref[...].astype(jnp.float32)
    label = lax.broadcasted_iota(jnp.int32, (ids.shape[0], LANES), 1)
    route = jnp.zeros((ids.shape[0], LANES), jnp.float32)
    for k in range(ids.shape[1]):
        route += jnp.where(ids[:, k : k + 1] == label, weights[:, k : k + 1], 0.0)
    out_ref[:, width:] = route.astype(out_ref.dtype)


def pack(tokens, expert_ids, gate_weights):
    rows, width = tokens.shape
    return pl.pallas_call(
        pack_kernel,
        in_specs=whole_vmem(3),
        out_specs=whole_vmem(1)[0],
        out_shape=VMEM((rows, width + LANES), tokens.dtype),
        compiler_params=pltpu.CompilerParams(vmem_limit_bytes=2 * 1024 * 1024),
    )(tokens, expert_ids, gate_weights)


def fetch_kernel(jobs, sources, *refs):
    src_refs = refs[:sources]
    out_refs = refs[sources + 1 : sources + 1 + len(jobs)]
    mark_ref, sems = refs[-2:]
    copies = []
    for n, (source, first, columns) in enumerate(jobs):
        rows = src_refs[source].shape[1]
        size = rows // 4
        for i in range(4):
            copies.append(
                pltpu.make_async_copy(
                    src_refs[source].at[0, pl.ds(i * size, size), pl.ds(first, columns)],
                    out_refs[n].at[pl.ds(i * size, size), :],
                    sems.at[n * 4 + i],
                )
            )
    for copy in copies:
        copy.start()
    mark_ref[...] = jnp.zeros_like(mark_ref)
    for copy in copies:
        copy.wait()


def fetch(jobs, weights, after):
    rows = weights[0].shape[1]
    shapes = [VMEM((rows, columns), weights[0].dtype) for _, _, columns in jobs]
    amount = sum(2 * rows * columns for _, _, columns in jobs)
    hbm = pl.BlockSpec(memory_space=pltpu.HBM)
    *out, mark = pl.pallas_call(
        functools.partial(fetch_kernel, jobs, len(weights)),
        in_specs=[hbm] * len(weights) + [pl.BlockSpec(memory_space=pl.ANY)],
        out_specs=whole_vmem(len(jobs) + 1),
        out_shape=shapes + [jax.ShapeDtypeStruct((8, LANES), jnp.float32)],
        scratch_shapes=[pltpu.SemaphoreType.DMA((4 * len(jobs),))],
        compiler_params=pltpu.CompilerParams(vmem_limit_bytes=1024 * 1024),
        cost_estimate=pl.CostEstimate(flops=0, bytes_accessed=amount, transcendentals=0),
    )(*[in_hbm(w) for w in weights], after)
    return out, mark


def join_kernel(count, *refs):
    rows = refs[0].shape[0]
    out_ref = refs[-1]
    out_ref[...] = jnp.concatenate(
        [r[...].astype(jnp.float32) for r in refs[:count]], axis=0
    ).astype(out_ref.dtype)


def join(values, after):
    rows, width = values[0].shape
    return pl.pallas_call(
        functools.partial(join_kernel, len(values)),
        in_specs=whole_vmem(len(values)) + [pl.BlockSpec(memory_space=pl.ANY)],
        out_specs=whole_vmem(1)[0],
        out_shape=VMEM((rows * len(values), width), values[0].dtype),
        compiler_params=pltpu.CompilerParams(vmem_limit_bytes=8 * 1024 * 1024),
    )(*[in_vmem(v) for v in values], after)


def expert_kernel(plan, share, *refs):
    parts, gate_at, up_at, streamed = plan
    x_refs, rest = refs[:parts], refs[parts:]
    held, rest = rest[: 1 + len(set(r for r, _ in gate_at + up_at if r is not None))], rest
    count = len(held) - 1
    w_refs = rest[:count]
    up_hbm, down_hbm, me_ref, own_ref, far_ref = rest[count : count + 5]
    flat, hidden, mix, up_ring, down_ring, up_sem, down_sem = rest[count + 5 :]
    width, units = flat.shape[1], hidden.shape[1]
    blocks = units // UNIT_BLOCK
    downs = width // DOWN_BLOCK

    def up_copy(n):
        first = streamed[n] * UNIT_BLOCK
        return pltpu.make_async_copy(
            up_hbm.at[0, :, pl.ds(first, UNIT_BLOCK)], up_ring.at[n % UP_RING], up_sem.at[n % UP_RING]
        )

    def down_copy(d, slot):
        first = d * DOWN_BLOCK
        if not isinstance(d, int):
            first = pl.multiple_of(first, DOWN_BLOCK)
        return pltpu.make_async_copy(
            down_hbm.at[0, :, pl.ds(first, DOWN_BLOCK)], down_ring.at[slot], down_sem.at[slot]
        )

    for n in range(min(UP_RING, len(streamed))):
        up_copy(n).start()
    for d in range(min(DOWN_RING, downs)):
        down_copy(d, d).start()

    route = jnp.concatenate([r[:, width:] for r in x_refs], axis=0)
    rows = route.shape[0]
    slots = flat.shape[0]
    lane = lax.broadcasted_iota(jnp.int32, (8, LANES), 1)
    pick = jnp.where(lane == me_ref[0], 1.0, 0.0).astype(jnp.bfloat16)
    weight = lax.dot_general(
        pick, route, (((1,), (1,)), ((), ())), preferred_element_type=jnp.float32
    )
    named = jnp.where(weight > 0.0, 1.0, 0.0)
    source = lax.broadcasted_iota(jnp.int32, (rows, rows), 0)
    target = lax.broadcasted_iota(jnp.int32, (rows, rows), 1)
    before = (source // share == target // share) & (source < target)
    rank = jnp.dot(
        named.astype(jnp.bfloat16),
        jnp.where(before, 1.0, 0.0).astype(jnp.bfloat16),
        preferred_element_type=jnp.float32,
    )
    token = lax.broadcasted_iota(jnp.int32, (1, rows), 1)
    slot = (token // share) * CAP + rank[:1].astype(jnp.int32)
    place = lax.broadcasted_iota(jnp.int32, (slots, rows), 0)
    chosen = (place == slot) & (named[:1] > 0.0)
    select = jnp.where(chosen, 1.0, 0.0).astype(jnp.bfloat16)
    mix[...] = jnp.transpose(jnp.where(chosen, weight[:1], 0.0)).astype(jnp.bfloat16)

    @pl.loop(0, downs)
    def _(d):
        columns = pl.ds(pl.multiple_of(d * DOWN_BLOCK, DOWN_BLOCK), DOWN_BLOCK)
        x = jnp.concatenate([r[:, columns] for r in x_refs], axis=0)
        flat[:, columns] = jnp.dot(
            select, x, preferred_element_type=jnp.float32
        ).astype(jnp.bfloat16)

    stream_of = {b: n for n, b in enumerate(streamed)}
    fixed = [b for b in range(blocks) if b not in stream_of]
    order = []
    waiting = list(streamed)
    for b in fixed:
        order.append(b)
        take = -(-len(waiting) // (len(fixed) - len(order) + sum(o in stream_of for o in order) + 1))
        order += waiting[:take]
        waiting = waiting[take:]
    order += waiting
    for b in order:
        where, first = gate_at[b]
        gate = jnp.dot(
            flat[...], w_refs[where][:, first : first + UNIT_BLOCK],
            preferred_element_type=jnp.float32,
        )
        if b in stream_of:
            n = stream_of[b]
            up_copy(n).wait()
            up = jnp.dot(
                flat[...], up_ring[n % UP_RING], preferred_element_type=jnp.float32
            )
            if n + UP_RING < len(streamed):
                up_copy(n + UP_RING).start()
        else:
            where, first = up_at[b]
            up = jnp.dot(
                flat[...], w_refs[where][:, first : first + UNIT_BLOCK],
                preferred_element_type=jnp.float32,
            )
        hidden[:, b * UNIT_BLOCK : (b + 1) * UNIT_BLOCK] = (jax.nn.silu(gate) * up).astype(
            jnp.bfloat16
        )

    @pl.loop(0, downs)
    def _(d):
        slot_of = lax.rem(d, DOWN_RING)
        columns = pl.ds(pl.multiple_of(d * DOWN_BLOCK, DOWN_BLOCK), DOWN_BLOCK)
        down_copy(d, slot_of).wait()
        part = jnp.dot(hidden[...], down_ring[slot_of], preferred_element_type=jnp.float32)

        @pl.when(d + DOWN_RING < downs)
        def _():
            down_copy(d + DOWN_RING, slot_of).start()

        spread = jnp.dot(
            mix[...], part.astype(jnp.bfloat16), preferred_element_type=jnp.float32
        ).astype(jnp.bfloat16)
        own_ref[:, columns] = spread[: rows // 2]
        far_ref[:, columns] = spread[rows // 2 :]


def hold_kernel(*refs):
    pass


def hold(values, after):
    out = pl.pallas_call(
        hold_kernel,
        in_specs=[pl.BlockSpec(memory_space=pl.ANY)] * (len(values) + 1),
        out_specs=[pl.BlockSpec(memory_space=pl.ANY)] * len(values),
        out_shape=[jax.ShapeDtypeStruct(v.shape, v.dtype) for v in values],
        input_output_aliases={i: i for i in range(len(values))},
    )(*values, after)
    return list(out)


def run_expert(parts, held, gate_at, up_at, streamed, w_up, w_down, me, share):
    rows = sum(p.shape[0] for p in parts)
    depth, units = w_up.shape[1], w_up.shape[2]
    slots = rows // share * CAP
    half = VMEM((rows // 2, depth), jnp.bfloat16)
    hbm = pl.BlockSpec(memory_space=pltpu.HBM)
    ring = max(1, min(UP_RING, len(streamed)))
    scratch = 2 * (
        slots * (depth + units) + rows * max(slots, LANES)
        + ring * depth * UNIT_BLOCK + DOWN_RING * units * DOWN_BLOCK
    )
    work = 4 * 1024 * 1024 + 10 * rows * rows
    return pl.pallas_call(
        functools.partial(expert_kernel, (len(parts), gate_at, up_at, streamed), share),
        in_specs=whole_vmem(len(parts) + len(held))
        + [hbm, hbm, pl.BlockSpec(memory_space=pltpu.SMEM)],
        out_specs=whole_vmem(2),
        out_shape=(half, half),
        scratch_shapes=[
            VMEM((slots, depth), jnp.bfloat16),
            VMEM((slots, units), jnp.bfloat16),
            VMEM((rows, slots), jnp.bfloat16),
            VMEM((ring, depth, UNIT_BLOCK), jnp.bfloat16),
            VMEM((DOWN_RING, units, DOWN_BLOCK), jnp.bfloat16),
            pltpu.SemaphoreType.DMA((ring,)),
            pltpu.SemaphoreType.DMA((DOWN_RING,)),
        ],
        compiler_params=pltpu.CompilerParams(vmem_limit_bytes=scratch + work),
        cost_estimate=pl.CostEstimate(
            flops=6 * slots * depth * units, bytes_accessed=4 * depth * units, transcendentals=0
        ),
    )(*[in_vmem(p) for p in parts], *[in_vmem(w) for w in held], in_hbm(w_up), in_hbm(w_down), me)


def add_kernel(count, *refs):
    ins, outs = refs[:count], refs[count:]
    total = ins[0][...].astype(jnp.float32)
    for ref in ins[1:]:
        total = total + ref[...].astype(jnp.float32)
    total = total.astype(jnp.bfloat16)
    size = total.shape[0] // len(outs)
    for i, ref in enumerate(outs):
        ref[...] = total[i * size : (i + 1) * size]


def add_split(values, pieces):
    rows, width = values[0].shape
    block = 1792
    out = jax.ShapeDtypeStruct((rows // pieces, width), jnp.bfloat16)
    return pl.pallas_call(
        functools.partial(add_kernel, len(values)),
        grid=(width // block,),
        in_specs=[pl.BlockSpec((rows, block), lambda i: (0, i))] * len(values),
        out_specs=(pl.BlockSpec((rows // pieces, block), lambda i: (0, i)),) * pieces,
        out_shape=(out,) * pieces,
        compiler_params=pltpu.CompilerParams(vmem_limit_bytes=24 * 1024 * 1024),
    )(*values)


def give_back(own, far, groups, members):
    lines = members // 2
    planes = add_split([own, other_core(far, members)], groups)
    planes = [planes[0]] + [shifted(planes[s], "group", groups, -s) for s in range(1, groups)]
    column = add_split(planes, lines)
    column = [column[0]] + [
        shifted(column[s], "expert", members, -s, 2) for s in range(1, lines)
    ]
    total = column[0].astype(jnp.float32)
    for value in column[1:]:
        total = total + value.astype(jnp.float32)
    return total.astype(jnp.bfloat16)


def on_device(tokens, expert_ids, gate_weights, w_gate, w_up, w_down):
    groups = lax.axis_size("group")
    members = lax.axis_size("expert")
    split = members // EXP_GRP
    lines = members // 2
    me = lax.axis_index("group") * EXP_GRP + lax.axis_index("expert") // split
    me = me.astype(jnp.int32).reshape(1)
    units = w_gate.shape[2]
    blocks = units // UNIT_BLOCK
    early = -(-blocks // 2)
    ups = max(1, 3 * blocks // 8)

    packed = pack(tokens, expert_ids, gate_weights)
    line = [packed] + [shifted(packed, "expert", members, s, 2) for s in range(1, lines)]
    held, mark = fetch([(0, 0, early * UNIT_BLOCK)], [w_gate], packed)
    column = join(line, mark)
    planes = [column] + [shifted(column, "group", groups, s) for s in range(1, groups)]
    jobs, sources = [], []
    if early < blocks:
        jobs.append((0, early * UNIT_BLOCK, (blocks - early) * UNIT_BLOCK))
        sources.append(w_gate)
    jobs.append((len(sources), 0, ups * UNIT_BLOCK))
    sources.append(w_up)
    more, mark = fetch(jobs, sources, column)
    held = held + more
    gate_at = [
        (0, b * UNIT_BLOCK) if b < early else (1, (b - early) * UNIT_BLOCK) for b in range(blocks)
    ]
    up_at = [
        (len(held) - 1, b * UNIT_BLOCK) if b < ups else (None, None) for b in range(blocks)
    ]
    planes = [column] + hold(planes[1:], mark)
    parts = planes + [other_core(p, members) for p in planes]
    own, far = run_expert(
        parts, held, gate_at, up_at, list(range(ups, blocks)), w_up, w_down, me, tokens.shape[0]
    )
    return give_back(own, far, groups, members)


def solution(mesh):
    in_specs = (
        P(AXES, None),
        P(AXES, None),
        P(AXES, None),
        P(AXES, None, None),
        P(AXES, None, None),
        P(AXES, None, None),
    )
    out_specs = P(AXES, None)
    return jax.shard_map(
        on_device, mesh=mesh, in_specs=in_specs, out_specs=out_specs, check_vma=False
    )
```

```python
import functools

import jax
import jax.numpy as jnp
from jax import lax
from jax.experimental import pallas as pl
from jax.experimental.pallas import tpu as pltpu
from jax.sharding import PartitionSpec as P

EXP_GRP = 8
LANES = 128
AXES = ("group", "expert")
VMEM = pltpu.VMEM
UNIT_BLOCK = 256
DOWN_BLOCK = 512
UP_RING = 2
DOWN_RING = 3
EARLY_DOWN = 2


def in_vmem(value):
    return pltpu.with_memory_space_constraint(value, VMEM)


def in_hbm(value):
    return pltpu.with_memory_space_constraint(value, pltpu.HBM)


def whole_vmem(count):
    return [pl.BlockSpec(memory_space=VMEM)] * count


def swap(value, axis, size, mask):
    return lax.ppermute(value, axis, [(i, i ^ mask) for i in range(size)])


def limit(amount):
    return pltpu.CompilerParams(vmem_limit_bytes=int(amount))


def cost(flops, amount):
    return pl.CostEstimate(flops=flops, bytes_accessed=amount, transcendentals=0)


def pack_kernel(tokens_ref, ids_ref, weights_ref, out_ref):
    width = tokens_ref.shape[1]
    out_ref[:, :width] = tokens_ref[...]
    ids = ids_ref[...]
    weights = weights_ref[...].astype(jnp.float32)
    label = lax.broadcasted_iota(jnp.int32, (ids.shape[0], LANES), 1)
    route = jnp.zeros((ids.shape[0], LANES), jnp.float32)
    for k in range(ids.shape[1]):
        route += jnp.where(ids[:, k : k + 1] == label, weights[:, k : k + 1], 0.0)
    out_ref[:, width:] = route.astype(out_ref.dtype)


def pack(tokens, expert_ids, gate_weights):
    rows, width = tokens.shape
    args = (tokens, expert_ids, gate_weights)
    return pl.pallas_call(
        pack_kernel,
        grid=(1,),
        in_specs=[pl.BlockSpec(a.shape, lambda i: (0, 0)) for a in args],
        out_specs=whole_vmem(1)[0],
        out_shape=VMEM((rows, width + LANES), tokens.dtype),
        compiler_params=limit(2 * 1024 * 1024),
    )(*[in_hbm(a) for a in args])


def fetch_kernel(jobs, *refs):
    src_refs = refs[: len(jobs)]
    out_refs = refs[len(jobs) + 1 : 2 * len(jobs) + 1]
    mark_ref, sems = refs[-2:]
    copies = []
    for n, (_, first, columns) in enumerate(jobs):
        size = src_refs[n].shape[1] // 4
        for i in range(4):
            copies.append(
                pltpu.make_async_copy(
                    src_refs[n].at[0, pl.ds(i * size, size), pl.ds(first, columns)],
                    out_refs[n].at[pl.ds(i * size, size), :],
                    sems.at[n * 4 + i],
                )
            )
    for copy in copies:
        copy.start()
    mark_ref[...] = jnp.zeros_like(mark_ref)
    for copy in copies:
        copy.wait()


def fetch(jobs, after):
    if not jobs:
        return [], None
    rows = jobs[0][0].shape[1]
    hbm = pl.BlockSpec(memory_space=pltpu.HBM)
    *out, mark = pl.pallas_call(
        functools.partial(fetch_kernel, jobs),
        in_specs=[hbm] * len(jobs) + [pl.BlockSpec(memory_space=pl.ANY)],
        out_specs=whole_vmem(len(jobs) + 1),
        out_shape=[VMEM((rows, columns), w.dtype) for w, _, columns in jobs]
        + [VMEM((8, LANES), jnp.float32)],
        scratch_shapes=[pltpu.SemaphoreType.DMA((4 * len(jobs),))],
        compiler_params=limit(256 * 1024),
        cost_estimate=cost(0, sum(2 * rows * columns for _, _, columns in jobs)),
    )(*[in_hbm(w) for w, _, _ in jobs], after)
    return out, mark


def join_kernel(cuts, first_ref, second_ref, after_ref, *out_refs):
    for (start, size), out_ref in zip(cuts, out_refs):
        columns = slice(start, start + size)
        halves = [r[:, columns].astype(jnp.float32) for r in (first_ref, second_ref)]
        out_ref[...] = jnp.concatenate(halves, axis=0).astype(out_ref.dtype)


def join(first, second, after, cuts=None):
    rows, width = first.shape
    cuts = cuts or [(0, width)]
    after = first if after is None else after
    return pl.pallas_call(
        functools.partial(join_kernel, cuts),
        in_specs=whole_vmem(2) + [pl.BlockSpec(memory_space=pl.ANY)],
        out_specs=whole_vmem(len(cuts)),
        out_shape=[VMEM((2 * rows, size), first.dtype) for _, size in cuts],
        compiler_params=limit(1024 * 1024 + 16 * rows * width),
    )(in_vmem(first), in_vmem(second), after)


def hold_kernel(*refs):
    pass


def hold(values, after):
    if after is None:
        return values
    return pl.pallas_call(
        hold_kernel,
        in_specs=[pl.BlockSpec(memory_space=pl.ANY)] * (len(values) + 1),
        out_specs=[pl.BlockSpec(memory_space=pl.ANY)] * len(values),
        out_shape=[jax.ShapeDtypeStruct(v.shape, v.dtype) for v in values],
        input_output_aliases={i: i for i in range(len(values))},
        compiler_params=limit(256 * 1024),
    )(*values, after)


def down_copier(down_hbm, ring, sems, start):
    def copy(d, slot):
        first = start + d * DOWN_BLOCK
        if not isinstance(d, int):
            first = pl.multiple_of(first, DOWN_BLOCK)
        return pltpu.make_async_copy(
            down_hbm.at[0, :, pl.ds(first, DOWN_BLOCK)], ring.at[slot], sems.at[slot]
        )

    return copy


def down_block(hidden_ref, weight, scale, own_ref, far_ref, columns):
    part = jnp.dot(hidden_ref[...], weight, preferred_element_type=jnp.float32)
    part = (part * scale).astype(jnp.bfloat16)
    half = part.shape[0] // 2
    own_ref[:, columns] = part[:half]
    far_ref[:, columns] = part[half:]


def down_loop(hidden_ref, ring, copy, scale_ref, own_ref, far_ref, first, downs):
    @pl.loop(first, downs)
    def _(d):
        slot = lax.rem(d, DOWN_RING)
        columns = pl.ds(pl.multiple_of(d * DOWN_BLOCK, DOWN_BLOCK), DOWN_BLOCK)
        copy(d, slot).wait()
        down_block(hidden_ref, ring[slot], scale_ref[:, :1], own_ref, far_ref, columns)

        @pl.when(d + DOWN_RING < downs)
        def _():
            copy(d + DOWN_RING, slot).start()


def expert_kernel(gate_at, up_at, streamed, held, *refs):
    a_refs, b_refs, refs = refs[:4], refs[4:8], refs[8:]
    w_refs, refs = refs[:held], refs[held:]
    up_hbm, down_hbm, me_ref, own_ref, far_ref, hidden, scale_ref, early_ref = refs[:8]
    x, up_ring, down_ring, up_sem, down_sem, early_sem = refs[8:]
    depth = x.shape[1]
    units = hidden.shape[1]
    width = own_ref.shape[1]
    blocks = units // UNIT_BLOCK
    downs = width // DOWN_BLOCK

    def up_copy(n):
        return pltpu.make_async_copy(
            up_hbm.at[0, :, pl.ds(streamed[n] * UNIT_BLOCK, UNIT_BLOCK)],
            up_ring.at[n % UP_RING],
            up_sem.at[n % UP_RING],
        )

    down_copy = down_copier(down_hbm, down_ring, down_sem, 0)
    early_copy = pltpu.make_async_copy(
        down_hbm.at[0, :, pl.ds(width, early_ref.shape[1])], early_ref, early_sem
    )
    later = {}
    for n in range(min(DOWN_RING, downs)):
        later.setdefault(min(blocks - 1, 2 + n), []).append(down_copy(n, n))
    later.setdefault(min(blocks - 1, 5), []).append(early_copy)

    for n in range(min(UP_RING, len(streamed))):
        up_copy(n).start()

    plane = a_refs[0].shape[0] // 2
    route = []
    for n, (a_ref, b_ref) in enumerate(zip(a_refs, b_refs)):
        core, pair = n // 2, n % 2
        for j in range(2):
            rows = slice(j * plane, (j + 1) * plane)
            at = core * 4 * plane + (2 * pair + j) * plane
            x[at : at + plane, :width] = a_ref[rows, :]
            at = core * 4 * plane + (2 * j + pair) * plane
            x[at : at + plane, width:] = b_ref[rows, :width]
            route.append((at, b_ref[rows, width:]))
    route = jnp.concatenate([r for _, r in sorted(route, key=lambda p: p[0])], axis=0)
    route = route.astype(jnp.float32)
    lane = lax.broadcasted_iota(jnp.int32, route.shape, 1)
    scale = jnp.sum(jnp.where(lane == me_ref[0], route, 0.0), axis=1, keepdims=True)
    scale_ref[...] = jnp.broadcast_to(scale, scale_ref.shape)

    def times(ref):
        return jnp.dot(x[...], ref[...], preferred_element_type=jnp.float32)

    for b in range(blocks):
        where, first = gate_at[b]
        gate = times(w_refs[where].at[:, first : first + UNIT_BLOCK])
        if up_at[b] is None:
            n = streamed.index(b)
            up_copy(n).wait()
            up = times(up_ring.at[n % UP_RING])
            if n + UP_RING < len(streamed):
                up_copy(n + UP_RING).start()
        else:
            where, first = up_at[b]
            up = times(w_refs[where].at[:, first : first + UNIT_BLOCK])
        for copy in later.get(b, []):
            copy.start()
        hidden[:, b * UNIT_BLOCK : (b + 1) * UNIT_BLOCK] = (jax.nn.silu(gate) * up).astype(
            jnp.bfloat16
        )
    down_loop(hidden, down_ring, down_copy, scale_ref, own_ref, far_ref, 0, downs)
    early_copy.wait()


def run_expert(a_parts, b_parts, held, gate_at, up_at, streamed, w_up, w_down, me):
    rows = sum(p.shape[0] for p in a_parts)
    depth, units = w_up.shape[1], w_up.shape[2]
    width = depth // 2
    half = VMEM((rows // 2, width), jnp.bfloat16)
    hbm = pl.BlockSpec(memory_space=pltpu.HBM)
    ring = max(1, min(UP_RING, len(streamed)))
    scratch = 2 * (rows * depth + ring * depth * UNIT_BLOCK + DOWN_RING * units * DOWN_BLOCK)
    work = 2816 * 1024 + 12 * rows * UNIT_BLOCK + 4 * rows * DOWN_BLOCK
    args = [in_vmem(v) for v in [*a_parts, *b_parts, *held]]
    return pl.pallas_call(
        functools.partial(expert_kernel, gate_at, up_at, streamed, len(held)),
        in_specs=whole_vmem(len(args)) + [hbm, hbm, pl.BlockSpec(memory_space=pltpu.SMEM)],
        out_specs=whole_vmem(5),
        out_shape=(
            half,
            half,
            VMEM((rows, units), jnp.bfloat16),
            VMEM((rows, LANES), jnp.float32),
            VMEM((units, EARLY_DOWN * DOWN_BLOCK), jnp.bfloat16),
        ),
        scratch_shapes=[
            VMEM((rows, depth), jnp.bfloat16),
            VMEM((ring, depth, UNIT_BLOCK), jnp.bfloat16),
            VMEM((DOWN_RING, units, DOWN_BLOCK), jnp.bfloat16),
            pltpu.SemaphoreType.DMA((ring,)),
            pltpu.SemaphoreType.DMA((DOWN_RING,)),
            pltpu.SemaphoreType.DMA,
        ],
        compiler_params=limit(scratch + work),
        cost_estimate=cost(5 * rows * depth * units, 4 * depth * units),
    )(*args, in_hbm(w_up), in_hbm(w_down), me)


def rest_kernel(hidden, scale_ref, early_ref, down_hbm, own_ref, far_ref, ring, sems):
    width = own_ref.shape[1]
    downs = width // DOWN_BLOCK
    copy = down_copier(down_hbm, ring, sems, width)
    for d in range(EARLY_DOWN, min(EARLY_DOWN + DOWN_RING, downs)):
        copy(d, d % DOWN_RING).start()
    for d in range(EARLY_DOWN):
        columns = slice(d * DOWN_BLOCK, (d + 1) * DOWN_BLOCK)
        down_block(hidden, early_ref[:, columns], scale_ref[:, :1], own_ref, far_ref, columns)
    down_loop(hidden, ring, copy, scale_ref, own_ref, far_ref, EARLY_DOWN, downs)


def run_rest(hidden, scale, early, w_down):
    rows, units = hidden.shape
    width = w_down.shape[2] // 2
    half = VMEM((rows // 2, width), jnp.bfloat16)
    scratch = 2 * DOWN_RING * units * DOWN_BLOCK
    work = 2 * 1024 * 1024 + 12 * rows * DOWN_BLOCK
    return pl.pallas_call(
        rest_kernel,
        in_specs=whole_vmem(3) + [pl.BlockSpec(memory_space=pltpu.HBM)],
        out_specs=whole_vmem(2),
        out_shape=(half, half),
        scratch_shapes=[
            VMEM((DOWN_RING, units, DOWN_BLOCK), jnp.bfloat16),
            pltpu.SemaphoreType.DMA((DOWN_RING,)),
        ],
        compiler_params=limit(scratch + work),
        cost_estimate=cost(2 * rows * width * units, 2 * width * units),
    )(in_vmem(hidden), in_vmem(scale), in_vmem(early), in_hbm(w_down))


def fold_kernel(picks, first_ref, second_ref, *out_refs):
    total = first_ref[...].astype(jnp.float32) + second_ref[...].astype(jnp.float32)
    for pick, out_ref in zip(picks, out_refs):
        pieces = [total[start : start + size] for start, size in pick]
        value = pieces[0] if len(pieces) == 1 else jnp.concatenate(pieces, axis=0)
        out_ref[...] = value.astype(out_ref.dtype)


def fold(first, second, picks):
    rows, width = first.shape
    return pl.pallas_call(
        functools.partial(fold_kernel, picks),
        in_specs=whole_vmem(2),
        out_specs=whole_vmem(len(picks)),
        out_shape=[VMEM((sum(n for _, n in pick), width), first.dtype) for pick in picks],
        compiler_params=limit(1024 * 1024 + 10 * rows * width),
    )(in_vmem(first), in_vmem(second))


def give_back(own, far, masks, groups, members):
    plane = own.shape[0] // 4
    keeps = [j for j in range(4) if not j & masks[0]]
    sends = [j for j in range(4) if j & masks[0]]
    picks = [[(j * plane, plane) for j in js] for js in (keeps, sends)]
    keep, send = fold(own, swap(far, "expert", members, 1), picks)
    for axis, size, mask in [
        ("group", groups, masks[0]),
        ("group", groups, masks[1]),
        *[("expert", members, 2 << k) for k in range((members // 2).bit_length() - 2)],
    ]:
        half = keep.shape[0] // 2
        keep, send = fold(keep, swap(send, axis, size, mask), [[(0, half)], [(half, half)]])
    got = swap(send, "expert", members, members // 2)
    return (keep.astype(jnp.float32) + got.astype(jnp.float32)).astype(jnp.bfloat16)


def on_device(tokens, expert_ids, gate_weights, w_gate, w_up, w_down):
    groups = lax.axis_size("group")
    members = lax.axis_size("expert")
    split = members // EXP_GRP
    me = lax.axis_index("group") * EXP_GRP + lax.axis_index("expert") // split
    me = me.astype(jnp.int32).reshape(1)
    width = tokens.shape[1] // 2
    blocks = w_gate.shape[2] // UNIT_BLOCK
    ups = max(1, blocks // 8)
    group = -(-blocks // 4)

    jobs, gate_at, count = [], [], 0
    for n in range(4):
        inside = list(range(n * group, min(blocks, (n + 1) * group)))
        job = []
        if inside:
            job.append((w_gate, inside[0] * UNIT_BLOCK, len(inside) * UNIT_BLOCK))
            gate_at += [(count, i * UNIT_BLOCK) for i in range(len(inside))]
            count += 1
        jobs.append(job)
    jobs[3].append((w_up, 0, ups * UNIT_BLOCK))
    up_at = [(count, b * UNIT_BLOCK) if b < ups else None for b in range(blocks)]
    streamed = list(range(ups, blocks))

    value = pack(tokens, expert_ids, gate_weights)
    held = []
    steps = [2 << k for k in reversed(range((members // 2).bit_length() - 1))]
    for n, mask in enumerate(steps):
        got = swap(value, "expert", members, mask)
        more, mark = fetch(jobs[n] if n < 2 else [], value)
        held += more
        if n < len(steps) - 1:
            (value,) = join(value, got, mark)
    a, b = join(value, got, mark, [(0, width), (width, width + LANES)])

    a_got, b_got = swap(a, "group", groups, 1), swap(b, "group", groups, 2)
    more, mark = fetch(jobs[2], a)
    held += more
    (a,) = join(a, a_got, mark)
    (b,) = join(b, b_got, mark)
    a_got, b_got = swap(a, "group", groups, 2), swap(b, "group", groups, 1)
    a_core, b_core = swap(a, "expert", members, 1), swap(b, "expert", members, 1)
    more, mark = fetch(jobs[3], a)
    held += more
    a_got, b_got = hold([a_got, b_got], mark)
    a_parts = [a, a_got, a_core, swap(a_got, "expert", members, 1)]
    b_parts = [b, b_got, b_core, swap(b_got, "expert", members, 1)]

    own, far, hidden, scale, early = run_expert(
        a_parts, b_parts, held, gate_at, up_at, streamed, w_up, w_down, me
    )
    left = give_back(own, far, (1, 2), groups, members)
    own, far = run_rest(hidden, scale, early, w_down)
    right = give_back(own, far, (2, 1), groups, members)
    return jnp.concatenate([left, right], axis=1)


def solution(mesh):
    in_specs = (
        P(AXES, None),
        P(AXES, None),
        P(AXES, None),
        P(AXES, None, None),
        P(AXES, None, None),
        P(AXES, None, None),
    )
    out_specs = P(AXES, None)
    return jax.shard_map(
        on_device, mesh=mesh, in_specs=in_specs, out_specs=out_specs, check_vma=False
    )
```

```python
import functools

import jax
import jax.numpy as jnp
from jax import lax
from jax.experimental import pallas as pl
from jax.experimental.pallas import tpu as pltpu
from jax.sharding import PartitionSpec as P

EXP_GRP = 8
LANES = 128
AXES = ("group", "expert")
VMEM = pltpu.VMEM
UNIT_BLOCK = 256
DOWN_BLOCK = 512
UP_RING = 3
DOWN_RING = 3
DEPTH_CUT = 1024


def in_vmem(value):
    return pltpu.with_memory_space_constraint(value, VMEM)


def in_hbm(value):
    return pltpu.with_memory_space_constraint(value, pltpu.HBM)


def whole_vmem(count):
    return [pl.BlockSpec(memory_space=VMEM)] * count


def swap(value, axis, size, mask):
    return lax.ppermute(value, axis, [(i, i ^ mask) for i in range(size)])


def swap_group(value, groups, members, masks):
    pairs = []
    for g in range(groups):
        for e in range(members):
            pairs.append((g * members + e, (g ^ masks[e % 2]) * members + e))
    return lax.ppermute(value, AXES, pairs)


def limit(amount):
    return pltpu.CompilerParams(vmem_limit_bytes=int(amount))


def cost(flops, amount):
    return pl.CostEstimate(flops=flops, bytes_accessed=amount, transcendentals=0)


def pack_kernel(me_ref, tokens_ref, ids_ref, weights_ref, out_ref):
    width = tokens_ref.shape[1]
    out_ref[:, :width] = tokens_ref[...]
    ids = ids_ref[...]
    weights = weights_ref[...].astype(jnp.float32)
    label = lax.broadcasted_iota(jnp.int32, (ids.shape[0], LANES), 1)
    route = jnp.zeros((ids.shape[0], LANES), jnp.float32)
    for k in range(ids.shape[1]):
        route += jnp.where(ids[:, k : k + 1] == label, weights[:, k : k + 1], 0.0)
    out_ref[:, width:] = route.astype(out_ref.dtype)


def pack(me, tokens, expert_ids, gate_weights):
    rows, width = tokens.shape
    args = (tokens, expert_ids, gate_weights)
    return pl.pallas_call(
        pack_kernel,
        grid=(1,),
        in_specs=[pl.BlockSpec(memory_space=pltpu.SMEM)]
        + [pl.BlockSpec(a.shape, lambda i: (0, 0)) for a in args],
        out_specs=whole_vmem(1)[0],
        out_shape=VMEM((rows, width + LANES), tokens.dtype),
        compiler_params=limit(2 * 1024 * 1024),
    )(me, *[in_hbm(a) for a in args])


def fetch_kernel(jobs, *refs):
    src_refs = refs[: len(jobs)]
    out_refs = refs[len(jobs) + 1 : 2 * len(jobs) + 1]
    mark_ref, sems = refs[-2:]
    copies = []
    for n, (_, first, columns) in enumerate(jobs):
        size = src_refs[n].shape[1] // 4
        for i in range(4):
            copies.append(
                pltpu.make_async_copy(
                    src_refs[n].at[0, pl.ds(i * size, size), pl.ds(first, columns)],
                    out_refs[n].at[pl.ds(i * size, size), :],
                    sems.at[n * 4 + i],
                )
            )
    for copy in copies:
        copy.start()
    mark_ref[...] = jnp.zeros_like(mark_ref)
    for copy in copies:
        copy.wait()


def fetch(jobs, after):
    if not jobs:
        return [], None
    rows = jobs[0][0].shape[1]
    hbm = pl.BlockSpec(memory_space=pltpu.HBM)
    *out, mark = pl.pallas_call(
        functools.partial(fetch_kernel, jobs),
        in_specs=[hbm] * len(jobs) + [pl.BlockSpec(memory_space=pl.ANY)],
        out_specs=whole_vmem(len(jobs) + 1),
        out_shape=[VMEM((rows, columns), w.dtype) for w, _, columns in jobs]
        + [VMEM((8, LANES), jnp.float32)],
        scratch_shapes=[pltpu.SemaphoreType.DMA((4 * len(jobs),))],
        compiler_params=limit(256 * 1024),
        cost_estimate=cost(0, sum(2 * rows * columns for _, _, columns in jobs)),
    )(*[in_hbm(w) for w, _, _ in jobs], after)
    return out, mark


def join_kernel(first_ref, second_ref, after_ref, out_ref):
    halves = [r[...].astype(jnp.float32) for r in (first_ref, second_ref)]
    out_ref[...] = jnp.concatenate(halves, axis=0).astype(out_ref.dtype)


def join(first, second, after):
    rows, width = first.shape
    after = first if after is None else after
    return pl.pallas_call(
        join_kernel,
        in_specs=whole_vmem(2) + [pl.BlockSpec(memory_space=pl.ANY)],
        out_specs=whole_vmem(1)[0],
        out_shape=VMEM((2 * rows, width), first.dtype),
        compiler_params=limit(1024 * 1024 + 16 * rows * width),
    )(in_vmem(first), in_vmem(second), after)


def hold_kernel(*refs):
    pass


def hold(value, after):
    if after is None:
        return value
    return pl.pallas_call(
        hold_kernel,
        in_specs=[pl.BlockSpec(memory_space=pl.ANY)] * 2,
        out_specs=pl.BlockSpec(memory_space=pl.ANY),
        out_shape=jax.ShapeDtypeStruct(value.shape, value.dtype),
        input_output_aliases={0: 0},
        compiler_params=limit(256 * 1024),
    )(value, after)


def times(left_ref, right_ref):
    depth = left_ref.shape[1]
    total = None
    for k in range(0, depth, DEPTH_CUT):
        inner = slice(k, min(depth, k + DEPTH_CUT))
        value = jnp.dot(left_ref[:, inner], right_ref[inner, :], preferred_element_type=jnp.float32)
        total = value if total is None else total + value
    return total


def expert_kernel(gate_at, up_at, streamed, held, *refs):
    x_refs, w_refs, refs = refs[:4], refs[4 : 4 + held], refs[4 + held :]
    up_hbm, down_hbm, me_ref, own_ref, far_ref = refs[:5]
    x, hidden, scale_ref, up_ring, down_ring, up_sem, down_sem = refs[5:]
    depth, units = x.shape[1], hidden.shape[1]
    blocks = units // UNIT_BLOCK
    downs = depth // DOWN_BLOCK

    def up_copy(n):
        return pltpu.make_async_copy(
            up_hbm.at[0, :, pl.ds(streamed[n] * UNIT_BLOCK, UNIT_BLOCK)],
            up_ring.at[n % UP_RING],
            up_sem.at[n % UP_RING],
        )

    def down_copy(d, slot):
        first = d * DOWN_BLOCK
        if not isinstance(d, int):
            first = pl.multiple_of(first, DOWN_BLOCK)
        return pltpu.make_async_copy(
            down_hbm.at[0, :, pl.ds(first, DOWN_BLOCK)], down_ring.at[slot], down_sem.at[slot]
        )

    later = {}
    for n in range(min(DOWN_RING, downs)):
        later.setdefault(min(blocks - 1, 2 + n), []).append(down_copy(n, n))
    for n in range(min(UP_RING, len(streamed))):
        up_copy(n).start()

    part = x_refs[0].shape[0]
    for n, x_ref in enumerate(x_refs):
        x[n * part : (n + 1) * part, :] = x_ref[:, :depth]
        route = x_ref[:, depth:].astype(jnp.float32)
        lane = lax.broadcasted_iota(jnp.int32, route.shape, 1)
        scale = jnp.sum(jnp.where(lane == me_ref[0], route, 0.0), axis=1, keepdims=True)
        scale_ref[n * part : (n + 1) * part, :] = jnp.broadcast_to(scale, route.shape)

    for b in range(blocks):
        where, first = gate_at[b]
        gate = times(x, w_refs[where].at[:, first : first + UNIT_BLOCK])
        if up_at[b] is None:
            n = streamed.index(b)
            up_copy(n).wait()
            up = times(x, up_ring.at[n % UP_RING])
            if n + UP_RING < len(streamed):
                up_copy(n + UP_RING).start()
        else:
            where, first = up_at[b]
            up = times(x, w_refs[where].at[:, first : first + UNIT_BLOCK])
        for copy in later.get(b, []):
            copy.start()
        hidden[:, b * UNIT_BLOCK : (b + 1) * UNIT_BLOCK] = (jax.nn.silu(gate) * up).astype(
            jnp.bfloat16
        )

    @pl.loop(0, downs)
    def _(d):
        slot = lax.rem(d, DOWN_RING)
        columns = pl.ds(pl.multiple_of(d * DOWN_BLOCK, DOWN_BLOCK), DOWN_BLOCK)
        down_copy(d, slot).wait()
        value = (times(hidden, down_ring.at[slot]) * scale_ref[:, :1]).astype(jnp.bfloat16)

        @pl.when(d + DOWN_RING < downs)
        def _():
            down_copy(d + DOWN_RING, slot).start()

        own_ref[:, columns] = value[: 2 * part]
        far_ref[:, columns] = value[2 * part :]


def run_expert(parts, held, gate_at, up_at, streamed, w_up, w_down, me):
    rows = sum(p.shape[0] for p in parts)
    depth, units = w_up.shape[1], w_up.shape[2]
    half = VMEM((rows // 2, depth), jnp.bfloat16)
    hbm = pl.BlockSpec(memory_space=pltpu.HBM)
    ring = max(1, min(UP_RING, len(streamed)))
    scratch = 2 * (
        rows * (depth + units + 2 * LANES)
        + ring * depth * UNIT_BLOCK
        + DOWN_RING * units * DOWN_BLOCK
    )
    work = 2560 * 1024 + 12 * rows * UNIT_BLOCK + 4 * rows * DOWN_BLOCK
    args = [in_vmem(v) for v in [*parts, *held]]
    return pl.pallas_call(
        functools.partial(expert_kernel, gate_at, up_at, streamed, len(held)),
        in_specs=whole_vmem(len(args)) + [hbm, hbm, pl.BlockSpec(memory_space=pltpu.SMEM)],
        out_specs=whole_vmem(2),
        out_shape=(half, half),
        scratch_shapes=[
            VMEM((rows, depth), jnp.bfloat16),
            VMEM((rows, units), jnp.bfloat16),
            VMEM((rows, LANES), jnp.float32),
            VMEM((ring, depth, UNIT_BLOCK), jnp.bfloat16),
            VMEM((DOWN_RING, units, DOWN_BLOCK), jnp.bfloat16),
            pltpu.SemaphoreType.DMA((ring,)),
            pltpu.SemaphoreType.DMA((DOWN_RING,)),
        ],
        compiler_params=limit(scratch + work),
        cost_estimate=cost(6 * rows * depth * units, 4 * depth * units),
    )(*args, in_hbm(w_up), in_hbm(w_down), me)


def fold_kernel(first_ref, second_ref, keep_ref, send_ref):
    total = first_ref[...].astype(jnp.float32) + second_ref[...].astype(jnp.float32)
    half = keep_ref.shape[0]
    keep_ref[...] = total[:half].astype(keep_ref.dtype)
    send_ref[...] = total[half:].astype(send_ref.dtype)


def fold(first, second):
    rows, width = first.shape
    return pl.pallas_call(
        fold_kernel,
        in_specs=whole_vmem(2),
        out_specs=whole_vmem(2),
        out_shape=[VMEM((rows // 2, width), first.dtype)] * 2,
        compiler_params=limit(1024 * 1024 + 10 * rows * width),
    )(in_vmem(first), in_vmem(second))


def give_back(own, far, groups, members):
    keep, send = fold(own, swap(far, "expert", members, 1))
    keep, send = fold(keep, swap_group(send, groups, members, (2, 1)))
    keep, send = fold(keep, swap_group(send, groups, members, (1, 2)))
    mask = 2
    while mask < members // 2:
        keep, send = fold(keep, swap(send, "expert", members, mask))
        mask *= 2
    got = swap(send, "expert", members, mask)
    return (keep.astype(jnp.float32) + got.astype(jnp.float32)).astype(jnp.bfloat16)


def on_device(tokens, expert_ids, gate_weights, w_gate, w_up, w_down):
    groups = lax.axis_size("group")
    members = lax.axis_size("expert")
    split = members // EXP_GRP
    me = lax.axis_index("group") * EXP_GRP + lax.axis_index("expert") // split
    me = me.astype(jnp.int32).reshape(1)
    blocks = w_gate.shape[2] // UNIT_BLOCK
    ups = max(1, blocks // 8)
    group = -(-blocks // 4)

    jobs, gate_at, count = [], [], 0
    for n in range(4):
        inside = list(range(n * group, min(blocks, (n + 1) * group)))
        job = []
        if inside:
            job.append((w_gate, inside[0] * UNIT_BLOCK, len(inside) * UNIT_BLOCK))
            gate_at += [(count, i * UNIT_BLOCK) for i in range(len(inside))]
            count += 1
        jobs.append(job)
    jobs[3].append((w_up, 0, ups * UNIT_BLOCK))
    up_at = [(count, b * UNIT_BLOCK) if b < ups else None for b in range(blocks)]
    streamed = list(range(ups, blocks))

    value = pack(me, tokens, expert_ids, gate_weights)
    held = []
    mask = members // 2
    number = 0
    while mask > 1:
        got = swap(value, "expert", members, mask)
        more, mark = fetch(jobs[number] if number < 2 else [], value)
        held += more
        value = join(value, got, mark)
        mask //= 2
        number += 1
    got = swap_group(value, groups, members, (1, 2))
    more, mark = fetch(jobs[2], value)
    held += more
    value = join(value, got, mark)
    got = swap_group(value, groups, members, (2, 1))
    core = swap(value, "expert", members, 1)
    more, mark = fetch(jobs[3], value)
    held += more
    got = hold(got, mark)
    parts = [value, got, core, swap(got, "expert", members, 1)]
    own, far = run_expert(parts, held, gate_at, up_at, streamed, w_up, w_down, me)
    return give_back(own, far, groups, members)


def solution(mesh):
    in_specs = (
        P(AXES, None),
        P(AXES, None),
        P(AXES, None),
        P(AXES, None, None),
        P(AXES, None, None),
        P(AXES, None, None),
    )
    out_specs = P(AXES, None)
    return jax.shard_map(
        on_device, mesh=mesh, in_specs=in_specs, out_specs=out_specs, check_vma=False
    )
```

```python
import functools

import jax
import jax.numpy as jnp
from jax import lax
from jax.experimental import pallas as pl
from jax.experimental.pallas import tpu as pltpu
from jax.sharding import PartitionSpec as P

EXP_GRP = 8
LANES = 128
AXES = ("group", "expert")
VMEM = pltpu.VMEM
FIRST_BLOCK = 512
UNIT_BLOCK = 256
DOWN_BLOCK = 512
EARLY = 2
RING = 6
DOWN_RING = 4
FOLD_BLOCK = 1024
DEPTH_CUT = 1024


def in_vmem(value):
    return pltpu.with_memory_space_constraint(value, VMEM)


def in_hbm(value):
    return pltpu.with_memory_space_constraint(value, pltpu.HBM)


def whole_vmem(count):
    return [pl.BlockSpec(memory_space=VMEM)] * count


def swap(value, axis, size, mask):
    return lax.ppermute(value, axis, [(i, i ^ mask) for i in range(size)])


def swap_group(value, groups, members, masks):
    pairs = []
    for g in range(groups):
        for e in range(members):
            pairs.append((g * members + e, (g ^ masks[e % 2]) * members + e))
    return lax.ppermute(value, AXES, pairs)


def limit(amount):
    return pltpu.CompilerParams(vmem_limit_bytes=int(amount))


def cost(flops, amount):
    return pl.CostEstimate(flops=flops, bytes_accessed=amount, transcendentals=0)


def pack_kernel(me_ref, tokens_ref, ids_ref, weights_ref, out_ref):
    width = tokens_ref.shape[1]
    out_ref[:, :width] = tokens_ref[...]
    ids = ids_ref[...]
    weights = weights_ref[...].astype(jnp.float32)
    label = lax.broadcasted_iota(jnp.int32, (ids.shape[0], LANES), 1)
    route = jnp.zeros((ids.shape[0], LANES), jnp.float32)
    for k in range(ids.shape[1]):
        route += jnp.where(ids[:, k : k + 1] == label, weights[:, k : k + 1], 0.0)
    out_ref[:, width:] = route.astype(out_ref.dtype)


def pack(me, tokens, expert_ids, gate_weights):
    rows, width = tokens.shape
    args = (tokens, expert_ids, gate_weights)
    return pl.pallas_call(
        pack_kernel,
        grid=(1,),
        in_specs=[pl.BlockSpec(memory_space=pltpu.SMEM)]
        + [pl.BlockSpec(a.shape, lambda i: (0, 0)) for a in args],
        out_specs=whole_vmem(1)[0],
        out_shape=VMEM((rows, width + LANES), tokens.dtype),
        compiler_params=limit(2 * 1024 * 1024),
    )(me, *[in_hbm(a) for a in args])


def fetch_kernel(jobs, *refs):
    src_refs = refs[: len(jobs)]
    out_refs = refs[len(jobs) + 1 : 2 * len(jobs) + 1]
    mark_ref, sems = refs[-2:]
    copies = []
    for n, (_, first, columns) in enumerate(jobs):
        size = out_refs[n].shape[0] // 4
        for i in range(4):
            copies.append(
                pltpu.make_async_copy(
                    src_refs[n].at[0, pl.ds(i * size, size), pl.ds(first, columns)],
                    out_refs[n].at[pl.ds(i * size, size), :],
                    sems.at[n * 4 + i],
                )
            )
    for copy in copies:
        copy.start()
    mark_ref[...] = jnp.zeros_like(mark_ref)
    for copy in copies:
        copy.wait()


def fetch(jobs, rows, after):
    hbm = pl.BlockSpec(memory_space=pltpu.HBM)
    *out, mark = pl.pallas_call(
        functools.partial(fetch_kernel, jobs),
        in_specs=[hbm] * len(jobs) + [pl.BlockSpec(memory_space=pl.ANY)],
        out_specs=whole_vmem(len(jobs) + 1),
        out_shape=[VMEM((rows, columns), w.dtype) for w, _, columns in jobs]
        + [VMEM((8, LANES), jnp.float32)],
        scratch_shapes=[pltpu.SemaphoreType.DMA((4 * len(jobs),))],
        compiler_params=limit(256 * 1024),
        cost_estimate=cost(0, sum(2 * rows * columns for _, _, columns in jobs)),
    )(*[in_hbm(w) for w, _, _ in jobs], after)
    return out, mark


def join_kernel(start, *refs):
    *in_refs, after_ref, out_ref = refs
    columns = slice(start, start + out_ref.shape[1])
    pieces = [r[:, columns].astype(jnp.float32) for r in in_refs]
    out_ref[...] = jnp.concatenate(pieces, axis=0).astype(out_ref.dtype)


def join(values, after, start=0, width=None):
    rows = sum(v.shape[0] for v in values)
    width = width or values[0].shape[1]
    after = values[0] if after is None else after
    return pl.pallas_call(
        functools.partial(join_kernel, start),
        in_specs=whole_vmem(len(values)) + [pl.BlockSpec(memory_space=pl.ANY)],
        out_specs=whole_vmem(1)[0],
        out_shape=VMEM((rows, width), values[0].dtype),
        compiler_params=limit(1024 * 1024 + 8 * rows * width),
    )(*[in_vmem(v) for v in values], after)


def hold_kernel(*refs):
    pass


def hold(value, after):
    return pl.pallas_call(
        hold_kernel,
        in_specs=[pl.BlockSpec(memory_space=pl.ANY)] * 2,
        out_specs=pl.BlockSpec(memory_space=pl.ANY),
        out_shape=jax.ShapeDtypeStruct(value.shape, value.dtype),
        input_output_aliases={0: 0},
        compiler_params=limit(256 * 1024),
    )(value, after)


def times(left_ref, right_ref):
    depth = left_ref.shape[1]
    total = None
    for k in range(0, depth, DEPTH_CUT):
        inner = slice(k, min(depth, k + DEPTH_CUT))
        value = jnp.dot(left_ref[:, inner], right_ref[inner, :], preferred_element_type=jnp.float32)
        total = value if total is None else total + value
    return total


def first_kernel(held, streams, early, *refs):
    x_refs, refs = refs[:4], refs[4:]
    held_refs, refs = refs[:held], refs[held:]
    hbm, after_ref, gate_ref, up_ref = refs[:2], *refs[2:5]
    early_refs, refs = refs[5 : 5 + len(early)], refs[5 + len(early) :]
    x, slots, stream_sem, early_sem = refs
    depth = x.shape[1]
    block = held_refs[0].shape[1]
    count = gate_ref.shape[1] // block

    copies = [
        pltpu.make_async_copy(
            hbm[m].at[0, pl.ds(0, depth), pl.ds(b * block, block)], slots.at[n], stream_sem.at[n]
        )
        for n, (m, b) in enumerate(streams)
    ]
    later = [
        pltpu.make_async_copy(
            hbm[m].at[0, pl.ds(depth, ref.shape[0]), pl.ds(b * UNIT_BLOCK, UNIT_BLOCK)],
            ref,
            early_sem.at[n],
        )
        for n, ((m, b), ref) in enumerate(zip(early, early_refs))
    ]
    for copy in copies:
        copy.start()
    part = x_refs[0].shape[0]
    for n, x_ref in enumerate(x_refs):
        x[n * part : (n + 1) * part, :] = x_ref[...]
    for n in range(2 * count):
        if n < held:
            weight = held_refs[n]
        else:
            copies[n - held].wait()
            weight = slots.at[n - held]
        out_ref = gate_ref if n < count else up_ref
        at = n % count * block
        out_ref[:, at : at + block] = times(x, weight)
        if n == min(1, 2 * count - 1):
            for copy in later:
                copy.start()
    for copy in later:
        copy.wait()


def run_first(parts, held, w_gate, w_up, after):
    rows = sum(p.shape[0] for p in parts)
    depth = parts[0].shape[1]
    units = w_gate.shape[2]
    block = held[0].shape[1]
    count = units // block
    order = [(0, b) for b in range(count)] + [(1, b) for b in range(count)]
    streams = order[len(held) :]
    early = [(m, b) for b in range(min(EARLY, units // UNIT_BLOCK)) for m in range(2)]
    hbm = pl.BlockSpec(memory_space=pltpu.HBM)
    slots = max(1, len(streams))
    scratch = 2 * (rows * depth + slots * depth * block)
    args = [in_vmem(v) for v in [*parts, *held]]
    return pl.pallas_call(
        functools.partial(first_kernel, len(held), streams, early),
        in_specs=whole_vmem(len(args)) + [hbm, hbm, pl.BlockSpec(memory_space=pl.ANY)],
        out_specs=whole_vmem(2 + len(early)),
        out_shape=[VMEM((rows, units), jnp.float32)] * 2
        + [VMEM((w_gate.shape[1] - depth, UNIT_BLOCK), w_gate.dtype)] * len(early),
        scratch_shapes=[
            VMEM((rows, depth), jnp.bfloat16),
            VMEM((slots, depth, block), jnp.bfloat16),
            pltpu.SemaphoreType.DMA((slots,)),
            pltpu.SemaphoreType.DMA((len(early),)),
        ],
        compiler_params=limit(scratch + 4 * 1024 * 1024 + 16 * rows * block),
        cost_estimate=cost(4 * rows * depth * units, 2 * depth * units),
    )(*args, in_hbm(w_gate), in_hbm(w_up), after)


def second_kernel(start, early, streams, *refs):
    x_refs, refs = refs[:4], refs[4:]
    gate_ref, up_ref, refs = refs[0], refs[1], refs[2:]
    early_refs, refs = refs[: len(early)], refs[len(early) :]
    hbm, down_hbm, me_ref, own_ref, far_ref = refs[:2], *refs[2:6]
    x, hidden, scale_ref, ring, down_ring, sems, down_sem = refs[6:]
    depth, units = x.shape[1], hidden.shape[1]
    blocks = units // UNIT_BLOCK
    downs = down_hbm.shape[2] // DOWN_BLOCK

    def copy(n):
        m, b = streams[n]
        return pltpu.make_async_copy(
            hbm[m].at[0, pl.ds(start, depth), pl.ds(b * UNIT_BLOCK, UNIT_BLOCK)],
            ring.at[n % RING],
            sems.at[n % RING],
        )

    def down_copy(d, slot):
        first = d * DOWN_BLOCK
        if not isinstance(d, int):
            first = pl.multiple_of(first, DOWN_BLOCK)
        return pltpu.make_async_copy(
            down_hbm.at[0, :, pl.ds(first, DOWN_BLOCK)], down_ring.at[slot], down_sem.at[slot]
        )

    for n in range(min(RING, len(streams))):
        copy(n).start()
    later = {}
    for n in range(min(DOWN_RING, downs)):
        later.setdefault(min(blocks - 1, 3 + n), []).append(down_copy(n, n))

    part = x_refs[0].shape[0]
    for n, x_ref in enumerate(x_refs):
        x[n * part : (n + 1) * part, :] = x_ref[:, :depth]
        route = x_ref[:, depth:].astype(jnp.float32)
        lane = lax.broadcasted_iota(jnp.int32, route.shape, 1)
        scale = jnp.sum(jnp.where(lane == me_ref[0], route, 0.0), axis=1, keepdims=True)
        scale_ref[n * part : (n + 1) * part, :] = jnp.broadcast_to(scale, route.shape)

    def product(m, b):
        if (m, b) in early:
            return times(x, early_refs[early.index((m, b))])
        n = streams.index((m, b))
        copy(n).wait()
        value = times(x, ring.at[n % RING])
        if n + RING < len(streams):
            copy(n + RING).start()
        return value

    for b in range(blocks):
        columns = slice(b * UNIT_BLOCK, (b + 1) * UNIT_BLOCK)
        gate = gate_ref[:, columns] + product(0, b)
        up = up_ref[:, columns] + product(1, b)
        for piece in later.get(b, []):
            piece.start()
        hidden[:, columns] = (jax.nn.silu(gate) * up).astype(jnp.bfloat16)

    @pl.loop(0, downs)
    def _(d):
        slot = lax.rem(d, DOWN_RING)
        columns = pl.ds(pl.multiple_of(d * DOWN_BLOCK, DOWN_BLOCK), DOWN_BLOCK)
        down_copy(d, slot).wait()
        value = (times(hidden, down_ring.at[slot]) * scale_ref[:, :1]).astype(jnp.bfloat16)

        @pl.when(d + DOWN_RING < downs)
        def _():
            down_copy(d + DOWN_RING, slot).start()

        own_ref[:, columns] = value[: 2 * part]
        far_ref[:, columns] = value[2 * part :]


def run_second(parts, gate, up, early_values, w_gate, w_up, w_down, me):
    rows = sum(p.shape[0] for p in parts)
    units, width = w_down.shape[1], w_down.shape[2]
    depth = parts[0].shape[1] - LANES
    blocks = units // UNIT_BLOCK
    order = [(m, b) for b in range(blocks) for m in range(2)]
    early = order[: len(early_values)]
    streams = order[len(early_values) :]
    half = VMEM((rows // 2, width), jnp.bfloat16)
    hbm = pl.BlockSpec(memory_space=pltpu.HBM)
    ring = max(1, min(RING, len(streams)))
    scratch = 2 * (
        rows * (depth + units + 2 * LANES)
        + ring * depth * UNIT_BLOCK
        + DOWN_RING * units * DOWN_BLOCK
    )
    args = [in_vmem(v) for v in [*parts, gate, up, *early_values]]
    return pl.pallas_call(
        functools.partial(second_kernel, width - depth, early, streams),
        in_specs=whole_vmem(len(args)) + [hbm] * 3 + [pl.BlockSpec(memory_space=pltpu.SMEM)],
        out_specs=whole_vmem(2),
        out_shape=(half, half),
        scratch_shapes=[
            VMEM((rows, depth), jnp.bfloat16),
            VMEM((rows, units), jnp.bfloat16),
            VMEM((rows, LANES), jnp.float32),
            VMEM((ring, depth, UNIT_BLOCK), jnp.bfloat16),
            VMEM((DOWN_RING, units, DOWN_BLOCK), jnp.bfloat16),
            pltpu.SemaphoreType.DMA((ring,)),
            pltpu.SemaphoreType.DMA((DOWN_RING,)),
        ],
        compiler_params=limit(scratch + 4 * 1024 * 1024 + 16 * rows * DOWN_BLOCK),
        cost_estimate=cost(2 * rows * units * (2 * depth + width), 2 * depth * units),
    )(*args, in_hbm(w_gate), in_hbm(w_up), in_hbm(w_down), me)


def fold_kernel(count, *refs):
    in_refs, out_refs = refs[:count], refs[count:]
    size = out_refs[0].shape[0]
    for first in range(0, in_refs[0].shape[1], FOLD_BLOCK):
        columns = slice(first, first + FOLD_BLOCK)
        total = in_refs[0][:, columns].astype(jnp.float32)
        for ref in in_refs[1:]:
            total = total + ref[:, columns].astype(jnp.float32)
        for n, ref in enumerate(out_refs):
            ref[:, columns] = total[n * size : (n + 1) * size].astype(ref.dtype)


def fold(values, pieces):
    rows, width = values[0].shape
    return pl.pallas_call(
        functools.partial(fold_kernel, len(values)),
        in_specs=whole_vmem(len(values)),
        out_specs=whole_vmem(pieces),
        out_shape=[VMEM((rows // pieces, width), values[0].dtype)] * pieces,
        compiler_params=limit(1024 * 1024 + 12 * rows * FOLD_BLOCK),
    )(*[in_vmem(v) for v in values])


def line_steps(lines):
    steps = []
    while lines > 1:
        radix = min(4, lines)
        lines //= radix
        steps.append([2 * lines * m for m in range(1, radix)])
    return steps


def give_back(own, far, groups, members):
    values = [own, swap(far, "expert", members, 1)]
    for masks in [(2, 1), (1, 2)]:
        keep, send = fold(values, 2)
        values = [keep, swap_group(send, groups, members, masks)]
    for masks in reversed(line_steps(members // 2)):
        keep, *sends = fold(values, len(masks) + 1)
        values = [keep] + [swap(v, "expert", members, m) for v, m in zip(sends, masks)]
    total = values[0].astype(jnp.float32)
    for value in values[1:]:
        total = total + value.astype(jnp.float32)
    return total.astype(jnp.bfloat16)


def on_device(tokens, expert_ids, gate_weights, w_gate, w_up, w_down):
    groups = lax.axis_size("group")
    members = lax.axis_size("expert")
    split = members // EXP_GRP
    me = lax.axis_index("group") * EXP_GRP + lax.axis_index("expert") // split
    me = me.astype(jnp.int32).reshape(1)
    depth, units = w_gate.shape[1], w_gate.shape[2]
    first = depth // DOWN_BLOCK * 3 // 8 * DOWN_BLOCK
    block = min(FIRST_BLOCK, units)
    jobs = [(w, at, block) for w in (w_gate, w_up) for at in range(0, units, block)]
    one = max(1, len(jobs) * 3 // 8)
    two = one + max(1, len(jobs) // 4)

    value = pack(me, tokens, expert_ids, gate_weights)
    held, mark = fetch(jobs[:one], first, value)
    for masks in line_steps(members // 2):
        line = [value] + [swap(value, "expert", members, m) for m in masks]
        if masks[0] > 2:
            value = join(line, mark)
    a = join(line, mark, 0, first)
    b = join(line, a, first, depth - first + LANES)

    a_got = swap_group(a, groups, members, (1, 2))
    b_got = swap_group(b, groups, members, (1, 2))
    a = join([a, a_got], b)
    b = join([b, b_got], a)
    a_got = swap_group(a, groups, members, (2, 1))
    b_got = swap_group(b, groups, members, (2, 1))
    more, mark = fetch(jobs[one:two], first, a)
    a_got = hold(a_got, mark)
    parts = [a, a_got, swap(a, "expert", members, 1), swap(a_got, "expert", members, 1)]
    gate, up, *early = run_first(parts, held + more, w_gate, w_up, b)
    b_got = hold(b_got, gate)
    parts = [b, b_got, swap(b, "expert", members, 1), swap(b_got, "expert", members, 1)]
    own, far = run_second(parts, gate, up, early, w_gate, w_up, w_down, me)
    return give_back(own, far, groups, members)


def solution(mesh):
    in_specs = (
        P(AXES, None),
        P(AXES, None),
        P(AXES, None),
        P(AXES, None, None),
        P(AXES, None, None),
        P(AXES, None, None),
    )
    out_specs = P(AXES, None)
    return jax.shard_map(
        on_device, mesh=mesh, in_specs=in_specs, out_specs=out_specs, check_vma=False
    )
```

```python
import functools

import jax
import jax.numpy as jnp
from jax import lax
from jax.experimental import pallas as pl
from jax.experimental.pallas import tpu as pltpu
from jax.sharding import PartitionSpec as P

EXP_GRP = 8
LANES = 128
AXES = ("group", "expert")
VMEM = pltpu.VMEM
UNIT_BLOCK = 256
DOWN_BLOCK = 512
UP_RING = 2
DOWN_RING = 5
FOLD_BLOCK = 1024
DEPTH_CUT = 1024


def in_vmem(value):
    return pltpu.with_memory_space_constraint(value, VMEM)


def in_hbm(value):
    return pltpu.with_memory_space_constraint(value, pltpu.HBM)


def whole_vmem(count):
    return [pl.BlockSpec(memory_space=VMEM)] * count


def swap(value, axis, size, mask):
    return lax.ppermute(value, axis, [(i, i ^ mask) for i in range(size)])


def swap_group(value, groups, members, masks):
    pairs = []
    for g in range(groups):
        for e in range(members):
            pairs.append((g * members + e, (g ^ masks[e % 2]) * members + e))
    return lax.ppermute(value, AXES, pairs)


def limit(amount):
    return pltpu.CompilerParams(vmem_limit_bytes=int(amount))


def cost(flops, amount):
    return pl.CostEstimate(flops=flops, bytes_accessed=amount, transcendentals=0)


def pack_kernel(me_ref, tokens_ref, ids_ref, weights_ref, out_ref):
    width = tokens_ref.shape[1]
    out_ref[:, :width] = tokens_ref[...]
    ids = ids_ref[...]
    weights = weights_ref[...].astype(jnp.float32)
    label = lax.broadcasted_iota(jnp.int32, (ids.shape[0], LANES), 1)
    route = jnp.zeros((ids.shape[0], LANES), jnp.float32)
    for k in range(ids.shape[1]):
        route += jnp.where(ids[:, k : k + 1] == label, weights[:, k : k + 1], 0.0)
    out_ref[:, width:] = route.astype(out_ref.dtype)


def pack(me, tokens, expert_ids, gate_weights):
    rows, width = tokens.shape
    args = (tokens, expert_ids, gate_weights)
    return pl.pallas_call(
        pack_kernel,
        grid=(1,),
        in_specs=[pl.BlockSpec(memory_space=pltpu.SMEM)]
        + [pl.BlockSpec(a.shape, lambda i: (0, 0)) for a in args],
        out_specs=whole_vmem(1)[0],
        out_shape=VMEM((rows, width + LANES), tokens.dtype),
        compiler_params=limit(2 * 1024 * 1024),
    )(me, *[in_hbm(a) for a in args])


def fetch_kernel(jobs, *refs):
    src_refs = refs[: len(jobs)]
    out_refs = refs[len(jobs) + 1 : 2 * len(jobs) + 1]
    mark_ref, sems = refs[-2:]
    copies = []
    for n, (_, first, columns) in enumerate(jobs):
        size = src_refs[n].shape[1] // 4
        for i in range(4):
            copies.append(
                pltpu.make_async_copy(
                    src_refs[n].at[0, pl.ds(i * size, size), pl.ds(first, columns)],
                    out_refs[n].at[pl.ds(i * size, size), :],
                    sems.at[n * 4 + i],
                )
            )
    for copy in copies:
        copy.start()
    mark_ref[...] = jnp.zeros_like(mark_ref)
    for copy in copies:
        copy.wait()


def fetch(jobs, after):
    if not jobs:
        return [], None
    rows = jobs[0][0].shape[1]
    hbm = pl.BlockSpec(memory_space=pltpu.HBM)
    *out, mark = pl.pallas_call(
        functools.partial(fetch_kernel, jobs),
        in_specs=[hbm] * len(jobs) + [pl.BlockSpec(memory_space=pl.ANY)],
        out_specs=whole_vmem(len(jobs) + 1),
        out_shape=[VMEM((rows, columns), w.dtype) for w, _, columns in jobs]
        + [VMEM((8, LANES), jnp.float32)],
        scratch_shapes=[pltpu.SemaphoreType.DMA((4 * len(jobs),))],
        compiler_params=limit(256 * 1024),
        cost_estimate=cost(0, sum(2 * rows * columns for _, _, columns in jobs)),
    )(*[in_hbm(w) for w, _, _ in jobs], after)
    return out, mark


def join_kernel(start, *refs):
    *in_refs, after_ref, out_ref = refs
    columns = slice(start, start + out_ref.shape[1])
    pieces = [r[:, columns].astype(jnp.float32) for r in in_refs]
    out_ref[...] = jnp.concatenate(pieces, axis=0).astype(out_ref.dtype)


def join(values, after, start=0, width=None):
    rows = sum(v.shape[0] for v in values)
    width = width or values[0].shape[1]
    after = values[0] if after is None else after
    return pl.pallas_call(
        functools.partial(join_kernel, start),
        in_specs=whole_vmem(len(values)) + [pl.BlockSpec(memory_space=pl.ANY)],
        out_specs=whole_vmem(1)[0],
        out_shape=VMEM((rows, width), values[0].dtype),
        compiler_params=limit(1024 * 1024 + 8 * rows * width),
    )(*[in_vmem(v) for v in values], after)


def hold_kernel(*refs):
    pass


def hold(value, after):
    if after is None:
        return value
    return pl.pallas_call(
        hold_kernel,
        in_specs=[pl.BlockSpec(memory_space=pl.ANY)] * 2,
        out_specs=pl.BlockSpec(memory_space=pl.ANY),
        out_shape=jax.ShapeDtypeStruct(value.shape, value.dtype),
        input_output_aliases={0: 0},
        compiler_params=limit(256 * 1024),
    )(value, after)


def times(left_ref, right_ref):
    depth = left_ref.shape[1]
    total = None
    for k in range(0, depth, DEPTH_CUT):
        inner = slice(k, min(depth, k + DEPTH_CUT))
        value = jnp.dot(left_ref[:, inner], right_ref[inner, :], preferred_element_type=jnp.float32)
        total = value if total is None else total + value
    return total


def expert_kernel(gate_at, up_at, streamed, held, *refs):
    x_refs, w_refs, refs = refs[:4], refs[4 : 4 + held], refs[4 + held :]
    up_hbm, down_hbm, me_ref, own_ref, far_ref = refs[:5]
    x, hidden, scale_ref, up_ring, down_ring, up_sem, down_sem = refs[5:]
    depth, units = x.shape[1], hidden.shape[1]
    blocks = units // UNIT_BLOCK
    downs = depth // DOWN_BLOCK

    def up_copy(n):
        return pltpu.make_async_copy(
            up_hbm.at[0, :, pl.ds(streamed[n] * UNIT_BLOCK, UNIT_BLOCK)],
            up_ring.at[n % UP_RING],
            up_sem.at[n % UP_RING],
        )

    def down_copy(d, slot):
        first = d * DOWN_BLOCK
        if not isinstance(d, int):
            first = pl.multiple_of(first, DOWN_BLOCK)
        return pltpu.make_async_copy(
            down_hbm.at[0, :, pl.ds(first, DOWN_BLOCK)], down_ring.at[slot], down_sem.at[slot]
        )

    later = {}
    for n in range(min(DOWN_RING, downs)):
        later.setdefault(min(blocks - 1, 1 + n), []).append(down_copy(n, n))
    for n in range(min(UP_RING, len(streamed))):
        up_copy(n).start()

    part = x_refs[0].shape[0]
    for n, x_ref in enumerate(x_refs):
        x[n * part : (n + 1) * part, :] = x_ref[:, :depth]
        route = x_ref[:, depth:].astype(jnp.float32)
        lane = lax.broadcasted_iota(jnp.int32, route.shape, 1)
        scale = jnp.sum(jnp.where(lane == me_ref[0], route, 0.0), axis=1, keepdims=True)
        scale_ref[n * part : (n + 1) * part, :] = jnp.broadcast_to(scale, route.shape)

    for b in range(blocks):
        where, first = gate_at[b]
        gate = times(x, w_refs[where].at[:, first : first + UNIT_BLOCK])
        if up_at[b] is None:
            n = streamed.index(b)
            up_copy(n).wait()
            up = times(x, up_ring.at[n % UP_RING])
            if n + UP_RING < len(streamed):
                up_copy(n + UP_RING).start()
        else:
            where, first = up_at[b]
            up = times(x, w_refs[where].at[:, first : first + UNIT_BLOCK])
        for copy in later.get(b, []):
            copy.start()
        hidden[:, b * UNIT_BLOCK : (b + 1) * UNIT_BLOCK] = (jax.nn.silu(gate) * up).astype(
            jnp.bfloat16
        )

    @pl.loop(0, downs)
    def _(d):
        slot = lax.rem(d, DOWN_RING)
        columns = pl.ds(pl.multiple_of(d * DOWN_BLOCK, DOWN_BLOCK), DOWN_BLOCK)
        down_copy(d, slot).wait()
        value = (times(hidden, down_ring.at[slot]) * scale_ref[:, :1]).astype(jnp.bfloat16)

        @pl.when(d + DOWN_RING < downs)
        def _():
            down_copy(d + DOWN_RING, slot).start()

        own_ref[:, columns] = value[: 2 * part]
        far_ref[:, columns] = value[2 * part :]


def run_expert(parts, held, gate_at, up_at, streamed, w_up, w_down, me):
    rows = sum(p.shape[0] for p in parts)
    depth, units = w_up.shape[1], w_up.shape[2]
    half = VMEM((rows // 2, depth), jnp.bfloat16)
    hbm = pl.BlockSpec(memory_space=pltpu.HBM)
    ring = max(1, min(UP_RING, len(streamed)))
    scratch = 2 * (
        rows * (depth + units + 2 * LANES)
        + ring * depth * UNIT_BLOCK
        + DOWN_RING * units * DOWN_BLOCK
    )
    work = 2560 * 1024 + 12 * rows * UNIT_BLOCK + 4 * rows * DOWN_BLOCK
    args = [in_vmem(v) for v in [*parts, *held]]
    return pl.pallas_call(
        functools.partial(expert_kernel, gate_at, up_at, streamed, len(held)),
        in_specs=whole_vmem(len(args)) + [hbm, hbm, pl.BlockSpec(memory_space=pltpu.SMEM)],
        out_specs=whole_vmem(2),
        out_shape=(half, half),
        scratch_shapes=[
            VMEM((rows, depth), jnp.bfloat16),
            VMEM((rows, units), jnp.bfloat16),
            VMEM((rows, LANES), jnp.float32),
            VMEM((ring, depth, UNIT_BLOCK), jnp.bfloat16),
            VMEM((DOWN_RING, units, DOWN_BLOCK), jnp.bfloat16),
            pltpu.SemaphoreType.DMA((ring,)),
            pltpu.SemaphoreType.DMA((DOWN_RING,)),
        ],
        compiler_params=limit(scratch + work),
        cost_estimate=cost(6 * rows * depth * units, 4 * depth * units),
    )(*args, in_hbm(w_up), in_hbm(w_down), me)


def fold_kernel(count, *refs):
    in_refs, out_refs = refs[:count], refs[count:]
    size = out_refs[0].shape[0]
    for first in range(0, in_refs[0].shape[1], FOLD_BLOCK):
        columns = slice(first, first + FOLD_BLOCK)
        total = in_refs[0][:, columns].astype(jnp.float32)
        for ref in in_refs[1:]:
            total = total + ref[:, columns].astype(jnp.float32)
        for n, ref in enumerate(out_refs):
            ref[:, columns] = total[n * size : (n + 1) * size].astype(ref.dtype)


def fold(values, pieces):
    rows, width = values[0].shape
    return pl.pallas_call(
        functools.partial(fold_kernel, len(values)),
        in_specs=whole_vmem(len(values)),
        out_specs=whole_vmem(pieces),
        out_shape=[VMEM((rows // pieces, width), values[0].dtype)] * pieces,
        compiler_params=limit(1024 * 1024 + 12 * rows * FOLD_BLOCK),
    )(*[in_vmem(v) for v in values])


def line_steps(lines):
    steps = []
    while lines > 1:
        radix = min(4, lines)
        lines //= radix
        steps.append([2 * lines * m for m in range(1, radix)])
    return steps


def give_back(own, far, groups, members):
    values = [own, swap(far, "expert", members, 1)]
    for masks in [(2, 1), (1, 2)]:
        keep, send = fold(values, 2)
        values = [keep, swap_group(send, groups, members, masks)]
    for masks in reversed(line_steps(members // 2)):
        keep, *sends = fold(values, len(masks) + 1)
        values = [keep] + [swap(v, "expert", members, m) for v, m in zip(sends, masks)]
    total = values[0].astype(jnp.float32)
    for value in values[1:]:
        total = total + value.astype(jnp.float32)
    return total.astype(jnp.bfloat16)


def on_device(tokens, expert_ids, gate_weights, w_gate, w_up, w_down):
    groups = lax.axis_size("group")
    members = lax.axis_size("expert")
    split = members // EXP_GRP
    me = lax.axis_index("group") * EXP_GRP + lax.axis_index("expert") // split
    me = me.astype(jnp.int32).reshape(1)
    blocks = w_gate.shape[2] // UNIT_BLOCK
    ups = max(1, blocks // 4)
    order = [(0, n) for n in range(blocks)] + [(1, n) for n in range(ups)]
    cuts = [len(order) * 3 // 10, len(order) * 6 // 10, len(order)]
    jobs, place = [], {}
    for start, stop in zip([0] + cuts, cuts):
        job = []
        for m in range(2):
            inside = [n for k, n in order[start:stop] if k == m]
            for i, n in enumerate(inside):
                place[m, n] = (sum(map(len, jobs)) + len(job), i * UNIT_BLOCK)
            if inside:
                weight = (w_gate, w_up)[m]
                job.append((weight, inside[0] * UNIT_BLOCK, len(inside) * UNIT_BLOCK))
        jobs.append(job)
    gate_at = [place[0, n] for n in range(blocks)]
    up_at = [place.get((1, n)) for n in range(blocks)]
    streamed = list(range(ups, blocks))

    value = pack(me, tokens, expert_ids, gate_weights)
    held, mark = fetch(jobs[0], value)
    for masks in line_steps(members // 2):
        line = [value] + [swap(value, "expert", members, m) for m in masks]
        value = join(line, mark)
    got = swap_group(value, groups, members, (1, 2))
    more, mark = fetch(jobs[1], value)
    held += more
    value = join([value, got], mark)
    got = swap_group(value, groups, members, (2, 1))
    core = swap(value, "expert", members, 1)
    more, mark = fetch(jobs[2], value)
    held += more
    got = hold(got, mark)
    parts = [value, got, core, swap(got, "expert", members, 1)]
    own, far = run_expert(parts, held, gate_at, up_at, streamed, w_up, w_down, me)
    return give_back(own, far, groups, members)


def solution(mesh):
    in_specs = (
        P(AXES, None),
        P(AXES, None),
        P(AXES, None),
        P(AXES, None, None),
        P(AXES, None, None),
        P(AXES, None, None),
    )
    out_specs = P(AXES, None)
    return jax.shard_map(
        on_device, mesh=mesh, in_specs=in_specs, out_specs=out_specs, check_vma=False
    )
```

```python
import functools

import jax
import jax.numpy as jnp
from jax import lax
from jax.experimental import pallas as pl
from jax.experimental.pallas import tpu as pltpu
from jax.sharding import PartitionSpec as P

EXP_GRP = 8
LANES = 128
AXES = ("group", "expert")
VMEM = pltpu.VMEM
UNIT_BLOCK = 256
DOWN_BLOCK = 512
RING = 4
DOWN_RING = 5
FOLD_BLOCK = 1024
DEPTH_CUT = 1024


def in_vmem(value):
    return pltpu.with_memory_space_constraint(value, VMEM)


def in_hbm(value):
    return pltpu.with_memory_space_constraint(value, pltpu.HBM)


def whole_vmem(count):
    return [pl.BlockSpec(memory_space=VMEM)] * count


def swap(value, axis, size, mask):
    return lax.ppermute(value, axis, [(i, i ^ mask) for i in range(size)])


def swap_group(value, groups, members, masks):
    pairs = []
    for g in range(groups):
        for e in range(members):
            pairs.append((g * members + e, (g ^ masks[e % 2]) * members + e))
    return lax.ppermute(value, AXES, pairs)


def limit(amount):
    return pltpu.CompilerParams(vmem_limit_bytes=int(amount))


def cost(flops, amount):
    return pl.CostEstimate(flops=flops, bytes_accessed=amount, transcendentals=0)


def pack_kernel(me_ref, tokens_ref, ids_ref, weights_ref, out_ref):
    width = tokens_ref.shape[1]
    out_ref[:, :width] = tokens_ref[...]
    ids = ids_ref[...]
    weights = weights_ref[...].astype(jnp.float32)
    label = lax.broadcasted_iota(jnp.int32, (ids.shape[0], LANES), 1)
    route = jnp.zeros((ids.shape[0], LANES), jnp.float32)
    for k in range(ids.shape[1]):
        route += jnp.where(ids[:, k : k + 1] == label, weights[:, k : k + 1], 0.0)
    out_ref[:, width:] = route.astype(out_ref.dtype)


def pack(me, tokens, expert_ids, gate_weights):
    rows, width = tokens.shape
    args = (tokens, expert_ids, gate_weights)
    return pl.pallas_call(
        pack_kernel,
        grid=(1,),
        in_specs=[pl.BlockSpec(memory_space=pltpu.SMEM)]
        + [pl.BlockSpec(a.shape, lambda i: (0, 0)) for a in args],
        out_specs=whole_vmem(1)[0],
        out_shape=VMEM((rows, width + LANES), tokens.dtype),
        compiler_params=limit(2 * 1024 * 1024),
    )(me, *[in_hbm(a) for a in args])


def fetch_kernel(jobs, *refs):
    src_refs = refs[: len(jobs)]
    out_refs = refs[len(jobs) + 1 : 2 * len(jobs) + 1]
    mark_ref, sems = refs[-2:]
    copies = []
    for n, (_, first, columns) in enumerate(jobs):
        size = src_refs[n].shape[1] // 4
        for i in range(4):
            copies.append(
                pltpu.make_async_copy(
                    src_refs[n].at[0, pl.ds(i * size, size), pl.ds(first, columns)],
                    out_refs[n].at[pl.ds(i * size, size), :],
                    sems.at[n * 4 + i],
                )
            )
    for copy in copies:
        copy.start()
    mark_ref[...] = jnp.zeros_like(mark_ref)
    for copy in copies:
        copy.wait()


def fetch(jobs, after):
    if not jobs:
        return [], None
    rows = jobs[0][0].shape[1]
    hbm = pl.BlockSpec(memory_space=pltpu.HBM)
    *out, mark = pl.pallas_call(
        functools.partial(fetch_kernel, jobs),
        in_specs=[hbm] * len(jobs) + [pl.BlockSpec(memory_space=pl.ANY)],
        out_specs=whole_vmem(len(jobs) + 1),
        out_shape=[VMEM((rows, columns), w.dtype) for w, _, columns in jobs]
        + [VMEM((8, LANES), jnp.float32)],
        scratch_shapes=[pltpu.SemaphoreType.DMA((4 * len(jobs),))],
        compiler_params=limit(256 * 1024),
        cost_estimate=cost(0, sum(2 * rows * columns for _, _, columns in jobs)),
    )(*[in_hbm(w) for w, _, _ in jobs], after)
    return out, mark


def join_kernel(cuts, *refs):
    in_refs, out_refs = refs[: -len(cuts) - 1], refs[-len(cuts) :]
    for (start, size), out_ref in zip(cuts, out_refs):
        pieces = [r[:, start : start + size].astype(jnp.float32) for r in in_refs]
        out_ref[...] = jnp.concatenate(pieces, axis=0).astype(out_ref.dtype)


def join(values, after, cuts=None):
    rows = sum(v.shape[0] for v in values)
    width = values[0].shape[1]
    cuts = cuts or [(0, width)]
    after = values[0] if after is None else after
    return pl.pallas_call(
        functools.partial(join_kernel, cuts),
        in_specs=whole_vmem(len(values)) + [pl.BlockSpec(memory_space=pl.ANY)],
        out_specs=whole_vmem(len(cuts)),
        out_shape=[VMEM((rows, size), values[0].dtype) for _, size in cuts],
        compiler_params=limit(1024 * 1024 + 8 * rows * width),
    )(*[in_vmem(v) for v in values], after)


def hold_kernel(*refs):
    pass


def hold(values, after):
    if after is None:
        return values
    return pl.pallas_call(
        hold_kernel,
        in_specs=[pl.BlockSpec(memory_space=pl.ANY)] * (len(values) + 1),
        out_specs=[pl.BlockSpec(memory_space=pl.ANY)] * len(values),
        out_shape=[jax.ShapeDtypeStruct(v.shape, v.dtype) for v in values],
        input_output_aliases={i: i for i in range(len(values))},
        compiler_params=limit(256 * 1024),
    )(*values, after)


def times(left_ref, right_ref):
    depth = left_ref.shape[1]
    total = None
    for k in range(0, depth, DEPTH_CUT):
        inner = slice(k, min(depth, k + DEPTH_CUT))
        value = jnp.dot(left_ref[:, inner], right_ref[inner, :], preferred_element_type=jnp.float32)
        total = value if total is None else total + value
    return total


def expert_kernel(place, order, streams, held, *refs):
    x_refs, w_refs, refs = refs[:8], refs[8 : 8 + held], refs[8 + held :]
    hbm, down_hbm, me_ref = refs[:2], refs[2], refs[3]
    own_refs, far_refs = refs[4:6], refs[6:8]
    x, hidden, scale_ref, ring, down_ring, sems, down_sem = refs[8:]
    depth, units = x.shape[1], hidden.shape[1]
    blocks = units // UNIT_BLOCK
    downs = depth // DOWN_BLOCK

    def copy(n):
        m, b = streams[n]
        return pltpu.make_async_copy(
            hbm[m].at[0, :, pl.ds(b * UNIT_BLOCK, UNIT_BLOCK)], ring.at[n % RING], sems.at[n % RING]
        )

    def down_copy(d, slot):
        return pltpu.make_async_copy(
            down_hbm.at[0, :, pl.ds(d * DOWN_BLOCK, DOWN_BLOCK)],
            down_ring.at[slot],
            down_sem.at[slot],
        )

    later = {}
    for n in range(min(DOWN_RING, downs)):
        later.setdefault(min(blocks - 1, 3 + n), []).append(down_copy(n, n))
    for n in range(min(RING, len(streams))):
        copy(n).start()

    part = x_refs[0].shape[0]
    width = depth // 2
    for n in range(4):
        rows = slice(n * part, (n + 1) * part)
        x[rows, :width] = x_refs[n][...]
        x[rows, width:] = x_refs[4 + n][:, :width]
        route = x_refs[4 + n][:, width:].astype(jnp.float32)
        lane = lax.broadcasted_iota(jnp.int32, route.shape, 1)
        scale = jnp.sum(jnp.where(lane == me_ref[0], route, 0.0), axis=1, keepdims=True)
        scale_ref[rows, :] = jnp.broadcast_to(scale, route.shape)

    def finish(b, gate, up):
        hidden[:, b * UNIT_BLOCK : (b + 1) * UNIT_BLOCK] = (jax.nn.silu(gate) * up).astype(
            jnp.bfloat16
        )

    waiting = None
    for turn, b in enumerate(order):
        weights, used = [], []
        for m in range(2):
            if (m, b) in place:
                where, first = place[m, b]
                weights.append(w_refs[where].at[:, first : first + UNIT_BLOCK])
            else:
                n = streams.index((m, b))
                copy(n).wait()
                weights.append(ring.at[n % RING])
                used.append(n)
        gate, up = [times(x, w) for w in weights]
        if waiting:
            finish(*waiting)
        waiting = (b, gate, up)
        for n in used:
            if n + RING < len(streams):
                copy(n + RING).start()
        for piece in later.get(turn, []):
            piece.start()
    finish(*waiting)

    for first in range(0, downs, 2):
        pair = range(first, min(first + 2, downs))
        for d in pair:
            down_copy(d, d % DOWN_RING).wait()
        for d in pair:
            value = times(hidden, down_ring.at[d % DOWN_RING]) * scale_ref[:, :1]
            value = value.astype(jnp.bfloat16)
            half, at = divmod(d * DOWN_BLOCK, width)
            own_refs[half][:, at : at + DOWN_BLOCK] = value[: 2 * part]
            far_refs[half][:, at : at + DOWN_BLOCK] = value[2 * part :]
        for d in pair:
            if d + DOWN_RING < downs:
                down_copy(d + DOWN_RING, d % DOWN_RING).start()


def run_expert(a_parts, b_parts, held, place, order, w_gate, w_up, w_down, me):
    rows = sum(p.shape[0] for p in a_parts)
    depth, units = w_up.shape[1], w_up.shape[2]
    half = VMEM((rows // 2, depth // 2), jnp.bfloat16)
    hbm = pl.BlockSpec(memory_space=pltpu.HBM)
    streams = [(m, b) for b in order for m in range(2) if (m, b) not in place]
    ring = max(1, min(RING, len(streams)))
    scratch = 2 * (
        rows * (depth + units + 2 * LANES)
        + ring * depth * UNIT_BLOCK
        + DOWN_RING * units * DOWN_BLOCK
    )
    work = 2560 * 1024 + 12 * rows * UNIT_BLOCK + 4 * rows * DOWN_BLOCK
    args = [in_vmem(v) for v in [*a_parts, *b_parts, *held]]
    return pl.pallas_call(
        functools.partial(expert_kernel, place, order, streams, len(held)),
        in_specs=whole_vmem(len(args)) + [hbm] * 3 + [pl.BlockSpec(memory_space=pltpu.SMEM)],
        out_specs=whole_vmem(4),
        out_shape=(half,) * 4,
        scratch_shapes=[
            VMEM((rows, depth), jnp.bfloat16),
            VMEM((rows, units), jnp.bfloat16),
            VMEM((rows, LANES), jnp.float32),
            VMEM((ring, depth, UNIT_BLOCK), jnp.bfloat16),
            VMEM((DOWN_RING, units, DOWN_BLOCK), jnp.bfloat16),
            pltpu.SemaphoreType.DMA((ring,)),
            pltpu.SemaphoreType.DMA((DOWN_RING,)),
        ],
        compiler_params=limit(scratch + work),
        cost_estimate=cost(6 * rows * depth * units, 4 * depth * units),
    )(*args, in_hbm(w_gate), in_hbm(w_up), in_hbm(w_down), me)


def fold_kernel(count, *refs):
    in_refs, out_refs = refs[:count], refs[count:]
    size = out_refs[0].shape[0]
    for first in range(0, in_refs[0].shape[1], FOLD_BLOCK):
        columns = slice(first, first + FOLD_BLOCK)
        total = in_refs[0][:, columns].astype(jnp.float32)
        for ref in in_refs[1:]:
            total = total + ref[:, columns].astype(jnp.float32)
        for n, ref in enumerate(out_refs):
            ref[:, columns] = total[n * size : (n + 1) * size].astype(ref.dtype)


def fold(values, pieces):
    rows, width = values[0].shape
    return pl.pallas_call(
        functools.partial(fold_kernel, len(values)),
        in_specs=whole_vmem(len(values)),
        out_specs=whole_vmem(pieces),
        out_shape=[VMEM((rows // pieces, width), values[0].dtype)] * pieces,
        compiler_params=limit(1024 * 1024 + 12 * rows * FOLD_BLOCK),
    )(*[in_vmem(v) for v in values])


def line_steps(lines):
    steps = []
    while lines > 1:
        radix = min(4, lines)
        lines //= radix
        steps.append([2 * lines * m for m in range(1, radix)])
    return steps


def give_back(own, far, groups, members):
    values = [own, swap(far, "expert", members, 1)]
    for masks in [(2, 1), (1, 2)]:
        keep, send = fold(values, 2)
        values = [keep, swap_group(send, groups, members, masks)]
    for masks in reversed(line_steps(members // 2)):
        keep, *sends = fold(values, len(masks) + 1)
        values = [keep] + [swap(v, "expert", members, m) for v, m in zip(sends, masks)]
    total = values[0].astype(jnp.float32)
    for value in values[1:]:
        total = total + value.astype(jnp.float32)
    return total.astype(jnp.bfloat16)


def on_device(tokens, expert_ids, gate_weights, w_gate, w_up, w_down):
    groups = lax.axis_size("group")
    members = lax.axis_size("expert")
    split = members // EXP_GRP
    me = lax.axis_index("group") * EXP_GRP + lax.axis_index("expert") // split
    me = me.astype(jnp.int32).reshape(1)
    blocks = w_gate.shape[2] // UNIT_BLOCK
    gates, ups = max(1, blocks // 2), max(1, blocks * 3 // 8)
    cuts = [0, max(1, gates // 2), max(1, gates * 3 // 4), gates]
    jobs, place, count = [], {}, 0
    for n in range(3):
        pieces = [(0, list(range(cuts[n], cuts[n + 1]))), (1, list(range(ups)) if n == 2 else [])]
        job = []
        for m, inside in pieces:
            if inside:
                job.append(((w_gate, w_up)[m], inside[0] * UNIT_BLOCK, len(inside) * UNIT_BLOCK))
                for i, b in enumerate(inside):
                    place[m, b] = (count, i * UNIT_BLOCK)
                count += 1
        jobs.append(job)
    order = list(range(min(2, ups)))
    fixed, loose = list(range(len(order), gates)), list(range(gates, blocks))
    while fixed or loose:
        order += loose[:1] + fixed[:1]
        fixed, loose = fixed[1:], loose[1:]

    value = pack(me, tokens, expert_ids, gate_weights)
    width = tokens.shape[1] // 2
    halves = [(0, width), (width, width + LANES)]
    held, mark = fetch(jobs[0], value)
    steps = line_steps(members // 2)
    for n, masks in enumerate(steps):
        line = [value] + [swap(value, "expert", members, m) for m in masks]
        value, *other = join(line, mark, halves if n == len(steps) - 1 else None)
    a, b = value, other[0]
    a_got, b_got = [swap_group(v, groups, members, (1, 2)) for v in (a, b)]
    more, mark = fetch(jobs[1], a)
    held += more
    (a,) = join([a, a_got], mark)
    (b,) = join([b, b_got], mark)
    a_got, b_got = [swap_group(v, groups, members, (2, 1)) for v in (a, b)]
    a_core, b_core = swap(a, "expert", members, 1), swap(b, "expert", members, 1)
    more, mark = fetch(jobs[2], a)
    held += more
    (a_got,), (b_got,) = hold([a_got], mark), hold([b_got], mark)
    a_parts = [a, a_got, a_core, swap(a_got, "expert", members, 1)]
    b_parts = [b, b_got, b_core, swap(b_got, "expert", members, 1)]
    sums = run_expert(a_parts, b_parts, held, place, order, w_gate, w_up, w_down, me)
    out = [give_back(own, far, groups, members) for own, far in zip(sums[:2], sums[2:])]
    return jnp.concatenate(out, axis=1)


def solution(mesh):
    in_specs = (
        P(AXES, None),
        P(AXES, None),
        P(AXES, None),
        P(AXES, None, None),
        P(AXES, None, None),
        P(AXES, None, None),
    )
    out_specs = P(AXES, None)
    return jax.shard_map(
        on_device, mesh=mesh, in_specs=in_specs, out_specs=out_specs, check_vma=False
    )
```

```python
import functools

import jax
import jax.numpy as jnp
from jax import lax
from jax.experimental import pallas as pl
from jax.experimental.pallas import tpu as pltpu
from jax.sharding import PartitionSpec as P

EXP_GRP = 8
LANES = 128
AXES = ("group", "expert")
VMEM = pltpu.VMEM
UNIT_BLOCK = 256
DOWN_BLOCK = 512
FIRST_BLOCK = 512
EARLY = 5
EARLY_DOWN = 3
RING = 4
DOWN_RING = 4
FOLD_BLOCK = 1024
DEPTH_CUT = 1024


def in_vmem(value):
    return pltpu.with_memory_space_constraint(value, VMEM)


def in_hbm(value):
    return pltpu.with_memory_space_constraint(value, pltpu.HBM)


def whole_vmem(count):
    return [pl.BlockSpec(memory_space=VMEM)] * count


def swap(value, axis, size, mask):
    return lax.ppermute(value, axis, [(i, i ^ mask) for i in range(size)])


def swap_group(value, groups, members, masks):
    pairs = []
    for g in range(groups):
        for e in range(members):
            pairs.append((g * members + e, (g ^ masks[e % 2]) * members + e))
    return lax.ppermute(value, AXES, pairs)


def limit(amount):
    return pltpu.CompilerParams(vmem_limit_bytes=int(amount))


def cost(flops, amount):
    return pl.CostEstimate(flops=flops, bytes_accessed=amount, transcendentals=0)


def pack_kernel(me_ref, tokens_ref, ids_ref, weights_ref, out_ref):
    width = tokens_ref.shape[1]
    out_ref[:, :width] = tokens_ref[...]
    ids = ids_ref[...]
    weights = weights_ref[...].astype(jnp.float32)
    label = lax.broadcasted_iota(jnp.int32, (ids.shape[0], LANES), 1)
    route = jnp.zeros((ids.shape[0], LANES), jnp.float32)
    for k in range(ids.shape[1]):
        route += jnp.where(ids[:, k : k + 1] == label, weights[:, k : k + 1], 0.0)
    out_ref[:, width:] = route.astype(out_ref.dtype)


def pack(me, tokens, expert_ids, gate_weights):
    rows, width = tokens.shape
    args = (tokens, expert_ids, gate_weights)
    return pl.pallas_call(
        pack_kernel,
        grid=(1,),
        in_specs=[pl.BlockSpec(memory_space=pltpu.SMEM)]
        + [pl.BlockSpec(a.shape, lambda i: (0, 0)) for a in args],
        out_specs=whole_vmem(1)[0],
        out_shape=VMEM((rows, width + LANES), tokens.dtype),
        compiler_params=limit(2 * 1024 * 1024),
    )(me, *[in_hbm(a) for a in args])


def fetch_kernel(jobs, *refs):
    src_refs = refs[: len(jobs)]
    out_refs = refs[len(jobs) + 1 : 2 * len(jobs) + 1]
    mark_ref, sems = refs[-2:]
    copies = []
    for n, (_, first, columns) in enumerate(jobs):
        size = out_refs[n].shape[0] // 4
        for i in range(4):
            copies.append(
                pltpu.make_async_copy(
                    src_refs[n].at[0, pl.ds(i * size, size), pl.ds(first, columns)],
                    out_refs[n].at[pl.ds(i * size, size), :],
                    sems.at[n * 4 + i],
                )
            )
    for copy in copies:
        copy.start()
    mark_ref[...] = jnp.zeros_like(mark_ref)
    for copy in copies:
        copy.wait()


def fetch(jobs, rows, after):
    if not jobs:
        return [], None
    hbm = pl.BlockSpec(memory_space=pltpu.HBM)
    *out, mark = pl.pallas_call(
        functools.partial(fetch_kernel, jobs),
        in_specs=[hbm] * len(jobs) + [pl.BlockSpec(memory_space=pl.ANY)],
        out_specs=whole_vmem(len(jobs) + 1),
        out_shape=[VMEM((rows, columns), w.dtype) for w, _, columns in jobs]
        + [VMEM((8, LANES), jnp.float32)],
        scratch_shapes=[pltpu.SemaphoreType.DMA((4 * len(jobs),))],
        compiler_params=limit(256 * 1024),
        cost_estimate=cost(0, sum(2 * rows * columns for _, _, columns in jobs)),
    )(*[in_hbm(w) for w, _, _ in jobs], after)
    return out, mark


def join_kernel(cuts, *refs):
    in_refs, out_refs = refs[: -len(cuts) - 1], refs[-len(cuts) :]
    for (start, size), out_ref in zip(cuts, out_refs):
        pieces = [r[:, start : start + size].astype(jnp.float32) for r in in_refs]
        out_ref[...] = jnp.concatenate(pieces, axis=0).astype(out_ref.dtype)


def join(values, after, cuts=None):
    rows = sum(v.shape[0] for v in values)
    width = values[0].shape[1]
    cuts = cuts or [(0, width)]
    after = values[0] if after is None else after
    return pl.pallas_call(
        functools.partial(join_kernel, cuts),
        in_specs=whole_vmem(len(values)) + [pl.BlockSpec(memory_space=pl.ANY)],
        out_specs=whole_vmem(len(cuts)),
        out_shape=[VMEM((rows, size), values[0].dtype) for _, size in cuts],
        compiler_params=limit(1024 * 1024 + 8 * rows * width),
    )(*[in_vmem(v) for v in values], after)


def hold_kernel(*refs):
    pass


def hold(values, after):
    if after is None:
        return values
    return pl.pallas_call(
        hold_kernel,
        in_specs=[pl.BlockSpec(memory_space=pl.ANY)] * (len(values) + 1),
        out_specs=[pl.BlockSpec(memory_space=pl.ANY)] * len(values),
        out_shape=[jax.ShapeDtypeStruct(v.shape, v.dtype) for v in values],
        input_output_aliases={i: i for i in range(len(values))},
        compiler_params=limit(256 * 1024),
    )(*values, after)


def times(left_ref, right_ref):
    depth = left_ref.shape[1]
    total = None
    for k in range(0, depth, DEPTH_CUT):
        inner = slice(k, min(depth, k + DEPTH_CUT))
        value = jnp.dot(left_ref[:, inner], right_ref[inner, :], preferred_element_type=jnp.float32)
        total = value if total is None else total + value
    return total


def first_kernel(held, streams, early, *refs):
    x_refs, refs = refs[:4], refs[4:]
    held_refs, refs = refs[:held], refs[held:]
    hbm, refs = refs[:2], refs[3:]
    gate_ref, up_ref, refs = refs[0], refs[1], refs[2:]
    early_refs, refs = refs[: len(early)], refs[len(early) :]
    x, slots, stream_sem, early_sem = refs
    depth = x.shape[1]
    block = slots.shape[2]
    count = gate_ref.shape[1] // block

    copies = [
        pltpu.make_async_copy(
            hbm[m].at[0, pl.ds(0, depth), pl.ds(b * block, block)], slots.at[n], stream_sem.at[n]
        )
        for n, (m, b) in enumerate(streams)
    ]
    later = [
        pltpu.make_async_copy(
            hbm[m].at[0, pl.ds(depth, ref.shape[0]), pl.ds(b * UNIT_BLOCK, UNIT_BLOCK)],
            ref,
            early_sem.at[n],
        )
        for n, ((m, b), ref) in enumerate(zip(early, early_refs))
    ]
    for copy in copies:
        copy.start()
    for copy in later[: len(later) // 2]:
        copy.start()
    part = x_refs[0].shape[0]
    for n, x_ref in enumerate(x_refs):
        x[n * part : (n + 1) * part, :] = x_ref[...]
    for n in range(2 * count):
        if n < held:
            weight = held_refs[n]
        else:
            copies[n - held].wait()
            weight = slots.at[n - held]
        out_ref = gate_ref if n < count else up_ref
        for at in range(0, block, UNIT_BLOCK):
            first = n % count * block + at
            out_ref[:, first : first + UNIT_BLOCK] = times(x, weight.at[:, at : at + UNIT_BLOCK])
        if n == min(2, 2 * count - 1):
            for copy in later[len(later) // 2 :]:
                copy.start()
    for copy in later:
        copy.wait()


def run_first(parts, held, w_gate, w_up, after):
    rows = sum(p.shape[0] for p in parts)
    depth = parts[0].shape[1]
    units = w_gate.shape[2]
    block = held[0].shape[1]
    count = units // block
    order = [(m, b) for m in range(2) for b in range(count)]
    streams = order[len(held) :]
    early = [(m, b) for b in range(min(EARLY, units // UNIT_BLOCK)) for m in range(2)]
    hbm = pl.BlockSpec(memory_space=pltpu.HBM)
    slots = max(1, len(streams))
    scratch = 2 * (rows * depth + slots * depth * block)
    args = [in_vmem(v) for v in [*parts, *held]]
    return pl.pallas_call(
        functools.partial(first_kernel, len(held), streams, early),
        in_specs=whole_vmem(len(args)) + [hbm, hbm, pl.BlockSpec(memory_space=pl.ANY)],
        out_specs=whole_vmem(2 + len(early)),
        out_shape=[VMEM((rows, units), jnp.float32)] * 2
        + [VMEM((w_gate.shape[1] - depth, UNIT_BLOCK), w_gate.dtype)] * len(early),
        scratch_shapes=[
            VMEM((rows, depth), jnp.bfloat16),
            VMEM((slots, depth, block), jnp.bfloat16),
            pltpu.SemaphoreType.DMA((slots,)),
            pltpu.SemaphoreType.DMA((len(early),)),
        ],
        compiler_params=limit(scratch + 2 * 1024 * 1024 + 16 * rows * UNIT_BLOCK),
        cost_estimate=cost(4 * rows * depth * units, 2 * depth * units),
    )(*args, in_hbm(w_gate), in_hbm(w_up), after)


def down_copier(down_hbm, ring, sems):
    def copy(d):
        return pltpu.make_async_copy(
            down_hbm.at[0, :, pl.ds(d * DOWN_BLOCK, DOWN_BLOCK)],
            ring.at[d % DOWN_RING],
            sems.at[d % DOWN_RING],
        )

    return copy


def down_blocks(hidden, scale_ref, weight_of, first, stop, own_ref, far_ref, after):
    half = own_ref.shape[0]
    for start in range(first, stop, 2):
        pair = range(start, min(start + 2, stop))
        weights = [weight_of(d) for d in pair]
        for d, weight in zip(pair, weights):
            value = (times(hidden, weight) * scale_ref[:, :1]).astype(jnp.bfloat16)
            at = (d - first) * DOWN_BLOCK
            own_ref[:, at : at + DOWN_BLOCK] = value[:half]
            far_ref[:, at : at + DOWN_BLOCK] = value[half:]
        for d in pair:
            after(d)


def second_kernel(start, early, streams, *refs):
    x_refs, refs = refs[:4], refs[4:]
    gate_ref, up_ref, refs = refs[0], refs[1], refs[2:]
    early_refs, refs = refs[: len(early)], refs[len(early) :]
    hbm, down_hbm, me_ref, refs = refs[:2], refs[2], refs[3], refs[4:]
    own_ref, far_ref, hidden, scale_ref, next_ref = refs[:5]
    x, ring, down_ring, sems, down_sem, next_sem = refs[5:]
    depth, units, width = x.shape[1], hidden.shape[1], own_ref.shape[1]
    blocks, downs = units // UNIT_BLOCK, width // DOWN_BLOCK

    def copy(n):
        m, b = streams[n]
        return pltpu.make_async_copy(
            hbm[m].at[0, pl.ds(start, depth), pl.ds(b * UNIT_BLOCK, UNIT_BLOCK)],
            ring.at[n % RING],
            sems.at[n % RING],
        )

    down_copy = down_copier(down_hbm, down_ring, down_sem)
    next_copy = pltpu.make_async_copy(
        down_hbm.at[0, :, pl.ds(width, next_ref.shape[1])], next_ref, next_sem
    )
    for n in range(min(RING, len(streams))):
        copy(n).start()
    later = {}
    for n in range(min(DOWN_RING, downs)):
        later.setdefault(min(blocks - 1, 1 + n), []).append(down_copy(n))

    part = x_refs[0].shape[0]
    for n, x_ref in enumerate(x_refs):
        rows = slice(n * part, (n + 1) * part)
        x[rows, :] = x_ref[:, :depth]
        route = x_ref[:, depth:].astype(jnp.float32)
        lane = lax.broadcasted_iota(jnp.int32, route.shape, 1)
        scale = jnp.sum(jnp.where(lane == me_ref[0], route, 0.0), axis=1, keepdims=True)
        scale_ref[rows, :] = jnp.broadcast_to(scale, route.shape)

    for b in range(blocks):
        columns = slice(b * UNIT_BLOCK, (b + 1) * UNIT_BLOCK)
        weights, used = [], []
        for m in range(2):
            if (m, b) in early:
                weights.append(early_refs[early.index((m, b))])
            else:
                n = streams.index((m, b))
                copy(n).wait()
                weights.append(ring.at[n % RING])
                used.append(n)
        gate = gate_ref[:, columns] + times(x, weights[0])
        up = up_ref[:, columns] + times(x, weights[1])
        for n in used:
            if n + RING < len(streams):
                copy(n + RING).start()
        for piece in later.get(b, []):
            piece.start()
        hidden[:, columns] = (jax.nn.silu(gate) * up).astype(jnp.bfloat16)

    def weight_of(d):
        down_copy(d).wait()
        return down_ring.at[d % DOWN_RING]

    def after(d):
        if d + DOWN_RING < downs:
            down_copy(d + DOWN_RING).start()
        if d == max(0, downs - DOWN_RING - 1):
            next_copy.start()

    down_blocks(hidden, scale_ref, weight_of, 0, downs, own_ref, far_ref, after)
    next_copy.wait()


def run_second(parts, gate, up, early_values, w_gate, w_up, w_down, me):
    rows = sum(p.shape[0] for p in parts)
    units, width = w_down.shape[1], w_down.shape[2]
    depth = parts[0].shape[1] - LANES
    order = [(m, b) for b in range(units // UNIT_BLOCK) for m in range(2)]
    early, streams = order[: len(early_values)], order[len(early_values) :]
    half = VMEM((rows // 2, width // 2), jnp.bfloat16)
    hbm = pl.BlockSpec(memory_space=pltpu.HBM)
    ring = max(1, min(RING, len(streams)))
    scratch = 2 * (
        rows * depth + ring * depth * UNIT_BLOCK + DOWN_RING * units * DOWN_BLOCK
    )
    args = [in_vmem(v) for v in [*parts, gate, up, *early_values]]
    return pl.pallas_call(
        functools.partial(second_kernel, width - depth, early, streams),
        in_specs=whole_vmem(len(args)) + [hbm] * 3 + [pl.BlockSpec(memory_space=pltpu.SMEM)],
        out_specs=whole_vmem(5),
        out_shape=(
            half,
            half,
            VMEM((rows, units), jnp.bfloat16),
            VMEM((rows, LANES), jnp.float32),
            VMEM((units, EARLY_DOWN * DOWN_BLOCK), w_down.dtype),
        ),
        scratch_shapes=[
            VMEM((rows, depth), jnp.bfloat16),
            VMEM((ring, depth, UNIT_BLOCK), jnp.bfloat16),
            VMEM((DOWN_RING, units, DOWN_BLOCK), jnp.bfloat16),
            pltpu.SemaphoreType.DMA((ring,)),
            pltpu.SemaphoreType.DMA((DOWN_RING,)),
            pltpu.SemaphoreType.DMA,
        ],
        compiler_params=limit(scratch + 2 * 1024 * 1024 + 16 * rows * DOWN_BLOCK),
        cost_estimate=cost(2 * rows * units * (2 * depth + width // 2), 2 * depth * units),
    )(*args, in_hbm(w_gate), in_hbm(w_up), in_hbm(w_down), me)


def third_kernel(hidden, scale_ref, next_ref, down_hbm, after_ref, own_ref, far_ref, ring, sems):
    downs = own_ref.shape[1] // DOWN_BLOCK
    copy = down_copier(down_hbm, ring, sems)
    resident = downs + EARLY_DOWN
    for d in range(resident, min(resident + DOWN_RING, 2 * downs)):
        copy(d).start()

    def weight_of(d):
        if d < resident:
            at = (d - downs) * DOWN_BLOCK
            return next_ref.at[:, at : at + DOWN_BLOCK]
        copy(d).wait()
        return ring.at[d % DOWN_RING]

    def after(d):
        if d >= resident and d + DOWN_RING < 2 * downs:
            copy(d + DOWN_RING).start()

    down_blocks(hidden, scale_ref, weight_of, downs, 2 * downs, own_ref, far_ref, after)


def run_third(hidden, scale, early, w_down, after):
    rows, units = hidden.shape
    width = w_down.shape[2] // 2
    half = VMEM((rows // 2, width), jnp.bfloat16)
    scratch = 2 * DOWN_RING * units * DOWN_BLOCK
    return pl.pallas_call(
        third_kernel,
        in_specs=whole_vmem(3)
        + [pl.BlockSpec(memory_space=pltpu.HBM), pl.BlockSpec(memory_space=pl.ANY)],
        out_specs=whole_vmem(2),
        out_shape=(half, half),
        scratch_shapes=[
            VMEM((DOWN_RING, units, DOWN_BLOCK), jnp.bfloat16),
            pltpu.SemaphoreType.DMA((DOWN_RING,)),
        ],
        compiler_params=limit(scratch + 2 * 1024 * 1024 + 16 * rows * DOWN_BLOCK),
        cost_estimate=cost(2 * rows * width * units, 2 * width * units),
    )(in_vmem(hidden), in_vmem(scale), in_vmem(early), in_hbm(w_down), after)


def fold_kernel(count, *refs):
    in_refs, out_refs = refs[:count], refs[count:]
    size = out_refs[0].shape[0]
    for first in range(0, in_refs[0].shape[1], FOLD_BLOCK):
        columns = slice(first, first + FOLD_BLOCK)
        total = in_refs[0][:, columns].astype(jnp.float32)
        for ref in in_refs[1:]:
            total = total + ref[:, columns].astype(jnp.float32)
        for n, ref in enumerate(out_refs):
            ref[:, columns] = total[n * size : (n + 1) * size].astype(ref.dtype)


def fold(values, pieces):
    rows, width = values[0].shape
    return pl.pallas_call(
        functools.partial(fold_kernel, len(values)),
        in_specs=whole_vmem(len(values)),
        out_specs=whole_vmem(pieces),
        out_shape=[VMEM((rows // pieces, width), values[0].dtype)] * pieces,
        compiler_params=limit(1024 * 1024 + 12 * rows * FOLD_BLOCK),
    )(*[in_vmem(v) for v in values])


def line_steps(lines):
    steps = []
    while lines > 1:
        radix = min(4, lines)
        lines //= radix
        steps.append([2 * lines * m for m in range(1, radix)])
    return steps


def chip_sum(own, far, members):
    return fold([own, swap(far, "expert", members, 1)], 2)


def give_back(keep, got, groups, members):
    keep, send = fold([keep, got], 2)
    values = [keep, swap_group(send, groups, members, (1, 2))]
    for masks in reversed(line_steps(members // 2)):
        keep, *sends = fold(values, len(masks) + 1)
        values = [keep] + [swap(v, "expert", members, m) for v, m in zip(sends, masks)]
    total = values[0].astype(jnp.float32)
    for value in values[1:]:
        total = total + value.astype(jnp.float32)
    return total.astype(jnp.bfloat16)


def on_device(tokens, expert_ids, gate_weights, w_gate, w_up, w_down):
    groups = lax.axis_size("group")
    members = lax.axis_size("expert")
    split = members // EXP_GRP
    me = lax.axis_index("group") * EXP_GRP + lax.axis_index("expert") // split
    me = me.astype(jnp.int32).reshape(1)
    width, units = w_gate.shape[1] // 2, w_gate.shape[2]
    block = min(FIRST_BLOCK, units)
    jobs = [(w, at, block) for w in (w_gate, w_up) for at in range(0, units, block)]
    cuts = [max(1, len(jobs) * 3 // 8), len(jobs) * 5 // 8, len(jobs) * 7 // 8]

    value = pack(me, tokens, expert_ids, gate_weights)
    held, mark = fetch(jobs[: cuts[0]], width, value)
    for masks in line_steps(members // 2):
        line = [value] + [swap(value, "expert", members, m) for m in masks]
        (value,) = join(line, mark)
    got = swap_group(value, groups, members, (1, 2))
    more, mark = fetch(jobs[cuts[0] : cuts[1]], width, value)
    held += more
    a, b = join([value, got], mark, [(0, width), (width, width + LANES)])
    a_got, b_got = [swap_group(v, groups, members, (2, 1)) for v in (a, b)]
    a_core, b_core = swap(a, "expert", members, 1), swap(b, "expert", members, 1)
    more, mark = fetch(jobs[cuts[1] : cuts[2]], width, a)
    held += more
    (a_got,) = hold([a_got], mark)
    parts = [a, a_got, a_core, swap(a_got, "expert", members, 1)]
    gate, up, *early = run_first(parts, held, w_gate, w_up, b)
    (b_got,) = hold([b_got], gate)
    parts = [b, b_got, b_core, swap(b_got, "expert", members, 1)]
    own, far, hidden, scale, early = run_second(
        parts, gate, up, early, w_gate, w_up, w_down, me
    )
    keep, send = chip_sum(own, far, members)
    got = swap_group(send, groups, members, (2, 1))
    own, far = run_third(hidden, scale, early, w_down, keep)
    (far,) = hold([far], got)
    left = give_back(keep, got, groups, members)
    keep, send = chip_sum(own, far, members)
    right = give_back(keep, swap_group(send, groups, members, (2, 1)), groups, members)
    return jnp.concatenate([left, right], axis=1)


def solution(mesh):
    in_specs = (
        P(AXES, None),
        P(AXES, None),
        P(AXES, None),
        P(AXES, None, None),
        P(AXES, None, None),
        P(AXES, None, None),
    )
    out_specs = P(AXES, None)
    return jax.shard_map(
        on_device, mesh=mesh, in_specs=in_specs, out_specs=out_specs, check_vma=False
    )
```

```python
import functools

import jax
import jax.numpy as jnp
from jax import lax
from jax.experimental import pallas as pl
from jax.experimental.pallas import tpu as pltpu
from jax.sharding import PartitionSpec as P

EXP_GRP = 8
LANES = 128
AXES = ("group", "expert")
VMEM = pltpu.VMEM
UNIT_BLOCK = 256
DOWN_BLOCK = 512
RING = 5
DOWN_RING = 5
FOLD_BLOCK = 1024


def in_vmem(value):
    return pltpu.with_memory_space_constraint(value, VMEM)


def in_hbm(value):
    return pltpu.with_memory_space_constraint(value, pltpu.HBM)


def whole_vmem(count):
    return [pl.BlockSpec(memory_space=VMEM)] * count


def swap(value, axis, size, mask):
    return lax.ppermute(value, axis, [(i, i ^ mask) for i in range(size)])


def swap_group(value, groups, members, masks):
    pairs = []
    for g in range(groups):
        for e in range(members):
            pairs.append((g * members + e, (g ^ masks[e % 2]) * members + e))
    return lax.ppermute(value, AXES, pairs)


def limit(amount):
    return pltpu.CompilerParams(vmem_limit_bytes=int(amount))


def cost(flops, amount):
    return pl.CostEstimate(flops=flops, bytes_accessed=amount, transcendentals=0)


def pack_kernel(me_ref, tokens_ref, ids_ref, weights_ref, out_ref):
    width = tokens_ref.shape[1]
    out_ref[:, :width] = tokens_ref[...]
    ids = ids_ref[...]
    weights = weights_ref[...].astype(jnp.float32)
    label = lax.broadcasted_iota(jnp.int32, (ids.shape[0], LANES), 1)
    route = jnp.zeros((ids.shape[0], LANES), jnp.float32)
    for k in range(ids.shape[1]):
        route += jnp.where(ids[:, k : k + 1] == label, weights[:, k : k + 1], 0.0)
    out_ref[:, width:] = route.astype(out_ref.dtype)


def pack(me, tokens, expert_ids, gate_weights):
    rows, width = tokens.shape
    args = (tokens, expert_ids, gate_weights)
    return pl.pallas_call(
        pack_kernel,
        grid=(1,),
        in_specs=[pl.BlockSpec(memory_space=pltpu.SMEM)]
        + [pl.BlockSpec(a.shape, lambda i: (0, 0)) for a in args],
        out_specs=whole_vmem(1)[0],
        out_shape=VMEM((rows, width + LANES), tokens.dtype),
        compiler_params=limit(2 * 1024 * 1024),
    )(me, *[in_hbm(a) for a in args])


def fetch_kernel(jobs, *refs):
    src_refs = refs[: len(jobs)]
    out_refs = refs[len(jobs) + 1 : 2 * len(jobs) + 1]
    mark_ref, sems = refs[-2:]
    copies = []
    for n, (_, first, columns) in enumerate(jobs):
        size = src_refs[n].shape[1] // 4
        for i in range(4):
            copies.append(
                pltpu.make_async_copy(
                    src_refs[n].at[0, pl.ds(i * size, size), pl.ds(first, columns)],
                    out_refs[n].at[pl.ds(i * size, size), :],
                    sems.at[n * 4 + i],
                )
            )
    for copy in copies:
        copy.start()
    mark_ref[...] = jnp.zeros_like(mark_ref)
    for copy in copies:
        copy.wait()


def fetch(jobs, after):
    if not jobs:
        return [], None
    rows = jobs[0][0].shape[1]
    hbm = pl.BlockSpec(memory_space=pltpu.HBM)
    *out, mark = pl.pallas_call(
        functools.partial(fetch_kernel, jobs),
        in_specs=[hbm] * len(jobs) + [pl.BlockSpec(memory_space=pl.ANY)],
        out_specs=whole_vmem(len(jobs) + 1),
        out_shape=[VMEM((rows, columns), w.dtype) for w, _, columns in jobs]
        + [VMEM((8, LANES), jnp.float32)],
        scratch_shapes=[pltpu.SemaphoreType.DMA((4 * len(jobs),))],
        compiler_params=limit(256 * 1024),
        cost_estimate=cost(0, sum(2 * rows * columns for _, _, columns in jobs)),
    )(*[in_hbm(w) for w, _, _ in jobs], after)
    return out, mark


def join_kernel(cuts, *refs):
    in_refs, out_refs = refs[: -len(cuts) - 1], refs[-len(cuts) :]
    for (start, size), out_ref in zip(cuts, out_refs):
        pieces = [r[:, start : start + size].astype(jnp.float32) for r in in_refs]
        out_ref[...] = jnp.concatenate(pieces, axis=0).astype(out_ref.dtype)


def join(values, after, cuts=None):
    rows = sum(v.shape[0] for v in values)
    width = values[0].shape[1]
    cuts = cuts or [(0, width)]
    after = values[0] if after is None else after
    return pl.pallas_call(
        functools.partial(join_kernel, cuts),
        in_specs=whole_vmem(len(values)) + [pl.BlockSpec(memory_space=pl.ANY)],
        out_specs=whole_vmem(len(cuts)),
        out_shape=[VMEM((rows, size), values[0].dtype) for _, size in cuts],
        compiler_params=limit(1024 * 1024 + 8 * rows * width),
    )(*[in_vmem(v) for v in values], after)


def hold_kernel(*refs):
    pass


def hold(values, after):
    if after is None:
        return values
    return pl.pallas_call(
        hold_kernel,
        in_specs=[pl.BlockSpec(memory_space=pl.ANY)] * (len(values) + 1),
        out_specs=[pl.BlockSpec(memory_space=pl.ANY)] * len(values),
        out_shape=[jax.ShapeDtypeStruct(v.shape, v.dtype) for v in values],
        input_output_aliases={i: i for i in range(len(values))},
        compiler_params=limit(256 * 1024),
    )(*values, after)


def times(left_ref, right_ref):
    return jnp.dot(left_ref[...], right_ref[...], preferred_element_type=jnp.float32)


def expert_kernel(place, order, streams, held, *refs):
    x_refs, w_refs, refs = refs[:8], refs[8 : 8 + held], refs[8 + held :]
    hbm, down_hbm, me_ref = refs[:2], refs[2], refs[3]
    own_refs, far_refs = refs[4:6], refs[6:8]
    x, hidden, scale_ref, ring, down_ring, sems, down_sem = refs[8:]
    depth, units = x.shape[1], hidden.shape[1]
    blocks = units // UNIT_BLOCK
    downs = depth // DOWN_BLOCK

    def copy(n):
        m, b = streams[n]
        return pltpu.make_async_copy(
            hbm[m].at[0, :, pl.ds(b * UNIT_BLOCK, UNIT_BLOCK)], ring.at[n % RING], sems.at[n % RING]
        )

    def down_copy(d, slot):
        return pltpu.make_async_copy(
            down_hbm.at[0, :, pl.ds(d * DOWN_BLOCK, DOWN_BLOCK)],
            down_ring.at[slot],
            down_sem.at[slot],
        )

    later = {}
    for n in range(min(DOWN_RING, downs)):
        later.setdefault(min(blocks - 1, 3 + n), []).append(down_copy(n, n))
    for n in range(min(RING, len(streams))):
        copy(n).start()

    part = x_refs[0].shape[0]
    width = depth // 2
    for n in range(4):
        rows = slice(n * part, (n + 1) * part)
        x[rows, :width] = x_refs[n][...]
        x[rows, width:] = x_refs[4 + n][:, :width]
        route = x_refs[4 + n][:, width:].astype(jnp.float32)
        lane = lax.broadcasted_iota(jnp.int32, route.shape, 1)
        scale = jnp.sum(jnp.where(lane == me_ref[0], route, 0.0), axis=1, keepdims=True)
        scale_ref[rows, :] = jnp.broadcast_to(scale, route.shape)

    def finish(b, gate, up):
        hidden[:, b * UNIT_BLOCK : (b + 1) * UNIT_BLOCK] = (jax.nn.silu(gate) * up).astype(
            jnp.bfloat16
        )

    waiting = None
    for turn, b in enumerate(order):
        weights, used = [], []
        for m in range(2):
            if (m, b) in place:
                where, first = place[m, b]
                weights.append(w_refs[where].at[:, first : first + UNIT_BLOCK])
            else:
                n = streams.index((m, b))
                copy(n).wait()
                weights.append(ring.at[n % RING])
                used.append(n)
        gate, up = [times(x, w) for w in weights]
        if waiting:
            finish(*waiting)
        waiting = (b, gate, up)
        for n in used:
            if n + RING < len(streams):
                copy(n + RING).start()
        for piece in later.get(turn, []):
            piece.start()
    finish(*waiting)

    for first in range(0, downs, 2):
        pair = range(first, min(first + 2, downs))
        for d in pair:
            down_copy(d, d % DOWN_RING).wait()
        for d in pair:
            value = times(hidden, down_ring.at[d % DOWN_RING]) * scale_ref[:, :1]
            value = value.astype(jnp.bfloat16)
            half, at = divmod(d * DOWN_BLOCK, width)
            own_refs[half][:, at : at + DOWN_BLOCK] = value[: 2 * part]
            far_refs[half][:, at : at + DOWN_BLOCK] = value[2 * part :]
        for d in pair:
            if d + DOWN_RING < downs:
                down_copy(d + DOWN_RING, d % DOWN_RING).start()


def run_expert(a_parts, b_parts, held, place, order, w_gate, w_up, w_down, me):
    rows = sum(p.shape[0] for p in a_parts)
    depth, units = w_up.shape[1], w_up.shape[2]
    half = VMEM((rows // 2, depth // 2), jnp.bfloat16)
    hbm = pl.BlockSpec(memory_space=pltpu.HBM)
    streams = [(m, b) for b in order for m in range(2) if (m, b) not in place]
    ring = max(1, min(RING, len(streams)))
    scratch = 2 * (
        rows * (depth + units + 2 * LANES)
        + ring * depth * UNIT_BLOCK
        + DOWN_RING * units * DOWN_BLOCK
    )
    work = 1024 * 1024 + 12 * rows * UNIT_BLOCK + 4 * rows * DOWN_BLOCK
    args = [in_vmem(v) for v in [*a_parts, *b_parts, *held]]
    return pl.pallas_call(
        functools.partial(expert_kernel, place, order, streams, len(held)),
        in_specs=whole_vmem(len(args)) + [hbm] * 3 + [pl.BlockSpec(memory_space=pltpu.SMEM)],
        out_specs=whole_vmem(4),
        out_shape=(half,) * 4,
        scratch_shapes=[
            VMEM((rows, depth), jnp.bfloat16),
            VMEM((rows, units), jnp.bfloat16),
            VMEM((rows, LANES), jnp.float32),
            VMEM((ring, depth, UNIT_BLOCK), jnp.bfloat16),
            VMEM((DOWN_RING, units, DOWN_BLOCK), jnp.bfloat16),
            pltpu.SemaphoreType.DMA((ring,)),
            pltpu.SemaphoreType.DMA((DOWN_RING,)),
        ],
        compiler_params=limit(scratch + work),
        cost_estimate=cost(6 * rows * depth * units, 4 * depth * units),
    )(*args, in_hbm(w_gate), in_hbm(w_up), in_hbm(w_down), me)


def fold_kernel(count, *refs):
    in_refs, out_refs = refs[:count], refs[count:]
    size = out_refs[0].shape[0]
    for first in range(0, in_refs[0].shape[1], FOLD_BLOCK):
        columns = slice(first, first + FOLD_BLOCK)
        total = in_refs[0][:, columns].astype(jnp.float32)
        for ref in in_refs[1:]:
            total = total + ref[:, columns].astype(jnp.float32)
        for n, ref in enumerate(out_refs):
            ref[:, columns] = total[n * size : (n + 1) * size].astype(ref.dtype)


def fold(values, pieces):
    rows, width = values[0].shape
    return pl.pallas_call(
        functools.partial(fold_kernel, len(values)),
        in_specs=whole_vmem(len(values)),
        out_specs=whole_vmem(pieces),
        out_shape=[VMEM((rows // pieces, width), values[0].dtype)] * pieces,
        compiler_params=limit(1024 * 1024 + 12 * rows * FOLD_BLOCK),
    )(*[in_vmem(v) for v in values])


def line_steps(lines):
    steps = []
    while lines > 1:
        radix = min(4, lines)
        lines //= radix
        steps.append([2 * lines * m for m in range(1, radix)])
    return steps


def give_back(own, far, groups, members):
    values = [own, swap(far, "expert", members, 1)]
    for masks in [(2, 1), (1, 2)]:
        keep, send = fold(values, 2)
        values = [keep, swap_group(send, groups, members, masks)]
    for masks in reversed(line_steps(members // 2)):
        keep, *sends = fold(values, len(masks) + 1)
        values = [keep] + [swap(v, "expert", members, m) for v, m in zip(sends, masks)]
    total = values[0].astype(jnp.float32)
    for value in values[1:]:
        total = total + value.astype(jnp.float32)
    return total.astype(jnp.bfloat16)


def on_device(tokens, expert_ids, gate_weights, w_gate, w_up, w_down):
    groups = lax.axis_size("group")
    members = lax.axis_size("expert")
    split = members // EXP_GRP
    me = lax.axis_index("group") * EXP_GRP + lax.axis_index("expert") // split
    me = me.astype(jnp.int32).reshape(1)
    blocks = w_gate.shape[2] // UNIT_BLOCK
    gates, ups = max(1, blocks // 2), max(1, blocks // 4)
    cuts = [0, max(1, gates * 3 // 4), gates, gates]
    jobs, place, count = [], {}, 0
    for n in range(3):
        pieces = [(0, list(range(cuts[n], cuts[n + 1]))), (1, list(range(ups)) if n == 2 else [])]
        job = []
        for m, inside in pieces:
            if inside:
                job.append(((w_gate, w_up)[m], inside[0] * UNIT_BLOCK, len(inside) * UNIT_BLOCK))
                for i, b in enumerate(inside):
                    place[m, b] = (count, i * UNIT_BLOCK)
                count += 1
        jobs.append(job)
    order = list(range(min(2, ups)))
    fixed, loose = list(range(len(order), gates)), list(range(gates, blocks))
    while fixed or loose:
        order += loose[:1] + fixed[:1]
        fixed, loose = fixed[1:], loose[1:]

    value = pack(me, tokens, expert_ids, gate_weights)
    width = tokens.shape[1] // 2
    halves = [(0, width), (width, width + LANES)]
    held, mark = fetch(jobs[0], value)
    steps = line_steps(members // 2)
    for n, masks in enumerate(steps):
        line = [value] + [swap(value, "expert", members, m) for m in masks]
        value, *other = join(line, mark, halves if n == len(steps) - 1 else None)
    a, b = value, other[0]
    a_got, b_got = [swap_group(v, groups, members, (1, 2)) for v in (a, b)]
    more, mark = fetch(jobs[1], a)
    held += more
    (a,) = join([a, a_got], mark)
    (b,) = join([b, b_got], mark)
    a_got, b_got = [swap_group(v, groups, members, (2, 1)) for v in (a, b)]
    a_core, b_core = swap(a, "expert", members, 1), swap(b, "expert", members, 1)
    more, mark = fetch(jobs[2], a)
    held += more
    (a_got,), (b_got,) = hold([a_got], mark), hold([b_got], mark)
    a_parts = [a, a_got, a_core, swap(a_got, "expert", members, 1)]
    b_parts = [b, b_got, b_core, swap(b_got, "expert", members, 1)]
    sums = run_expert(a_parts, b_parts, held, place, order, w_gate, w_up, w_down, me)
    out = [give_back(own, far, groups, members) for own, far in zip(sums[:2], sums[2:])]
    return jnp.concatenate(out, axis=1)


def solution(mesh):
    in_specs = (
        P(AXES, None),
        P(AXES, None),
        P(AXES, None),
        P(AXES, None, None),
        P(AXES, None, None),
        P(AXES, None, None),
    )
    out_specs = P(AXES, None)
    return jax.shard_map(
        on_device, mesh=mesh, in_specs=in_specs, out_specs=out_specs, check_vma=False
    )
```

```python
import functools

import jax
import jax.numpy as jnp
from jax import lax
from jax.experimental import pallas as pl
from jax.experimental.pallas import tpu as pltpu
from jax.sharding import PartitionSpec as P

EXP_GRP = 8
LANES = 128
AXES = ("group", "expert")
VMEM = pltpu.VMEM
UNIT_BLOCK = 256
DOWN_BLOCK = 512
RING = 3
DOWN_RING = 5
FOLD_BLOCK = 1024


def in_vmem(value):
    return pltpu.with_memory_space_constraint(value, VMEM)


def in_hbm(value):
    return pltpu.with_memory_space_constraint(value, pltpu.HBM)


def whole_vmem(count):
    return [pl.BlockSpec(memory_space=VMEM)] * count


def swap(value, axis, size, masks):
    masks = masks if isinstance(masks, tuple) else (masks, masks)
    return lax.ppermute(value, axis, [(i, i ^ masks[i % 2]) for i in range(size)])


def swap_group(value, groups, members, masks):
    pairs = []
    for g in range(groups):
        for e in range(members):
            pairs.append((g * members + e, (g ^ masks[e % 2]) * members + e))
    return lax.ppermute(value, AXES, pairs)


def limit(amount):
    return pltpu.CompilerParams(vmem_limit_bytes=int(amount))


def cost(flops, amount):
    return pl.CostEstimate(flops=flops, bytes_accessed=amount, transcendentals=0)


def pack_kernel(me_ref, tokens_ref, ids_ref, weights_ref, out_ref):
    width = tokens_ref.shape[1]
    out_ref[:, :width] = tokens_ref[...]
    ids = ids_ref[...]
    weights = weights_ref[...].astype(jnp.float32)
    label = lax.broadcasted_iota(jnp.int32, (ids.shape[0], LANES), 1)
    route = jnp.zeros((ids.shape[0], LANES), jnp.float32)
    for k in range(ids.shape[1]):
        route += jnp.where(ids[:, k : k + 1] == label, weights[:, k : k + 1], 0.0)
    out_ref[:, width:] = route.astype(out_ref.dtype)


def pack(me, tokens, expert_ids, gate_weights):
    rows, width = tokens.shape
    args = (tokens, expert_ids, gate_weights)
    return pl.pallas_call(
        pack_kernel,
        grid=(1,),
        in_specs=[pl.BlockSpec(memory_space=pltpu.SMEM)]
        + [pl.BlockSpec(a.shape, lambda i: (0, 0)) for a in args],
        out_specs=whole_vmem(1)[0],
        out_shape=VMEM((rows, width + LANES), tokens.dtype),
        compiler_params=limit(2 * 1024 * 1024),
    )(me, *[in_hbm(a) for a in args])


def fetch_kernel(jobs, *refs):
    src_refs = refs[: len(jobs)]
    out_refs = refs[len(jobs) + 1 : 2 * len(jobs) + 1]
    mark_ref, sems = refs[-2:]
    copies = []
    for n, (_, first, columns) in enumerate(jobs):
        size = src_refs[n].shape[1] // 4
        for i in range(4):
            copies.append(
                pltpu.make_async_copy(
                    src_refs[n].at[0, pl.ds(i * size, size), pl.ds(first, columns)],
                    out_refs[n].at[pl.ds(i * size, size), :],
                    sems.at[n * 4 + i],
                )
            )
    for copy in copies:
        copy.start()
    mark_ref[...] = jnp.zeros_like(mark_ref)
    for copy in copies:
        copy.wait()


def fetch(jobs, after):
    if not jobs:
        return [], None
    rows = jobs[0][0].shape[1]
    hbm = pl.BlockSpec(memory_space=pltpu.HBM)
    *out, mark = pl.pallas_call(
        functools.partial(fetch_kernel, jobs),
        in_specs=[hbm] * len(jobs) + [pl.BlockSpec(memory_space=pl.ANY)],
        out_specs=whole_vmem(len(jobs) + 1),
        out_shape=[VMEM((rows, columns), w.dtype) for w, _, columns in jobs]
        + [VMEM((8, LANES), jnp.float32)],
        scratch_shapes=[pltpu.SemaphoreType.DMA((4 * len(jobs),))],
        compiler_params=limit(256 * 1024),
        cost_estimate=cost(0, sum(2 * rows * columns for _, _, columns in jobs)),
    )(*[in_hbm(w) for w, _, _ in jobs], after)
    return out, mark


def join_kernel(cuts, *refs):
    in_refs, out_refs = refs[: -len(cuts) - 1], refs[-len(cuts) :]
    for (start, size), out_ref in zip(cuts, out_refs):
        pieces = [r[:, start : start + size].astype(jnp.float32) for r in in_refs]
        out_ref[...] = jnp.concatenate(pieces, axis=0).astype(out_ref.dtype)


def join(values, after, cuts=None):
    rows = sum(v.shape[0] for v in values)
    width = values[0].shape[1]
    cuts = cuts or [(0, width)]
    after = values[0] if after is None else after
    return pl.pallas_call(
        functools.partial(join_kernel, cuts),
        in_specs=whole_vmem(len(values)) + [pl.BlockSpec(memory_space=pl.ANY)],
        out_specs=whole_vmem(len(cuts)),
        out_shape=[VMEM((rows, size), values[0].dtype) for _, size in cuts],
        compiler_params=limit(1024 * 1024 + 8 * rows * width),
    )(*[in_vmem(v) for v in values], after)


def hold_kernel(*refs):
    pass


def hold(values, after):
    if after is None:
        return values
    return pl.pallas_call(
        hold_kernel,
        in_specs=[pl.BlockSpec(memory_space=pl.ANY)] * (len(values) + 1),
        out_specs=[pl.BlockSpec(memory_space=pl.ANY)] * len(values),
        out_shape=[jax.ShapeDtypeStruct(v.shape, v.dtype) for v in values],
        input_output_aliases={i: i for i in range(len(values))},
        compiler_params=limit(256 * 1024),
    )(*values, after)


def times(left_ref, right_ref):
    return jnp.dot(left_ref[...], right_ref[...], preferred_element_type=jnp.float32)


def expert_kernel(place, order, streams, held, *refs):
    x_refs, w_refs, refs = refs[:8], refs[8 : 8 + held], refs[8 + held :]
    hbm, down_hbm, me_ref = refs[:2], refs[2], refs[3]
    own_refs, far_refs = refs[4:6], refs[6:8]
    x, hidden, scale_ref, ring, down_ring, sems, down_sem = refs[8:]
    depth, units = x.shape[1], hidden.shape[1]
    blocks = units // UNIT_BLOCK
    downs = depth // DOWN_BLOCK

    def copy(n):
        m, b = streams[n]
        return pltpu.make_async_copy(
            hbm[m].at[0, :, pl.ds(b * UNIT_BLOCK, UNIT_BLOCK)], ring.at[n % RING], sems.at[n % RING]
        )

    def down_copy(d, slot):
        return pltpu.make_async_copy(
            down_hbm.at[0, :, pl.ds(d * DOWN_BLOCK, DOWN_BLOCK)],
            down_ring.at[slot],
            down_sem.at[slot],
        )

    later = {}
    for n in range(min(DOWN_RING, downs)):
        later.setdefault(min(blocks - 1, 3 + n), []).append(down_copy(n, n))
    for n in range(min(RING, len(streams))):
        copy(n).start()

    part = x_refs[0].shape[0]
    width = depth // 2
    for n in range(4):
        rows = slice(n * part, (n + 1) * part)
        x[rows, :width] = x_refs[n][...]
        x[rows, width:] = x_refs[4 + n][:, :width]
        route = x_refs[4 + n][:, width:].astype(jnp.float32)
        lane = lax.broadcasted_iota(jnp.int32, route.shape, 1)
        scale = jnp.sum(jnp.where(lane == me_ref[0], route, 0.0), axis=1, keepdims=True)
        scale_ref[rows, :] = jnp.broadcast_to(scale, route.shape)

    def finish(b, gate, up):
        hidden[:, b * UNIT_BLOCK : (b + 1) * UNIT_BLOCK] = (jax.nn.silu(gate) * up).astype(
            jnp.bfloat16
        )

    waiting = None
    for turn, b in enumerate(order):
        weights, used = [], []
        for m in range(2):
            if (m, b) in place:
                where, first = place[m, b]
                weights.append(w_refs[where].at[:, first : first + UNIT_BLOCK])
            else:
                n = streams.index((m, b))
                copy(n).wait()
                weights.append(ring.at[n % RING])
                used.append(n)
        gate, up = [times(x, w) for w in weights]
        if waiting:
            finish(*waiting)
        waiting = (b, gate, up)
        for n in used:
            if n + RING < len(streams):
                copy(n + RING).start()
        for piece in later.get(turn, []):
            piece.start()
    finish(*waiting)

    for first in range(0, downs, 2):
        pair = range(first, min(first + 2, downs))
        for d in pair:
            down_copy(d, d % DOWN_RING).wait()
        for d in pair:
            value = times(hidden, down_ring.at[d % DOWN_RING]) * scale_ref[:, :1]
            value = value.astype(jnp.bfloat16)
            half, at = divmod(d * DOWN_BLOCK, width)
            own_refs[half][:, at : at + DOWN_BLOCK] = value[: 2 * part]
            far_refs[half][:, at : at + DOWN_BLOCK] = value[2 * part :]
        for d in pair:
            if d + DOWN_RING < downs:
                down_copy(d + DOWN_RING, d % DOWN_RING).start()


def run_expert(a_parts, b_parts, held, place, order, w_gate, w_up, w_down, me):
    rows = sum(p.shape[0] for p in a_parts)
    depth, units = w_up.shape[1], w_up.shape[2]
    half = VMEM((rows // 2, depth // 2), jnp.bfloat16)
    hbm = pl.BlockSpec(memory_space=pltpu.HBM)
    streams = [(m, b) for b in order for m in range(2) if (m, b) not in place]
    ring = max(1, min(RING, len(streams)))
    scratch = 2 * (
        rows * (depth + units + 2 * LANES)
        + ring * depth * UNIT_BLOCK
        + DOWN_RING * units * DOWN_BLOCK
    )
    work = 1024 * 1024 + 12 * rows * UNIT_BLOCK + 4 * rows * DOWN_BLOCK
    args = [in_vmem(v) for v in [*a_parts, *b_parts, *held]]
    return pl.pallas_call(
        functools.partial(expert_kernel, place, order, streams, len(held)),
        in_specs=whole_vmem(len(args)) + [hbm] * 3 + [pl.BlockSpec(memory_space=pltpu.SMEM)],
        out_specs=whole_vmem(4),
        out_shape=(half,) * 4,
        scratch_shapes=[
            VMEM((rows, depth), jnp.bfloat16),
            VMEM((rows, units), jnp.bfloat16),
            VMEM((rows, LANES), jnp.float32),
            VMEM((ring, depth, UNIT_BLOCK), jnp.bfloat16),
            VMEM((DOWN_RING, units, DOWN_BLOCK), jnp.bfloat16),
            pltpu.SemaphoreType.DMA((ring,)),
            pltpu.SemaphoreType.DMA((DOWN_RING,)),
        ],
        compiler_params=limit(scratch + work),
        cost_estimate=cost(6 * rows * depth * units, 4 * depth * units),
    )(*args, in_hbm(w_gate), in_hbm(w_up), in_hbm(w_down), me)


def fold_kernel(count, *refs):
    in_refs, out_refs = refs[:count], refs[count:]
    size = out_refs[0].shape[0]
    for first in range(0, in_refs[0].shape[1], FOLD_BLOCK):
        columns = slice(first, first + FOLD_BLOCK)
        total = in_refs[0][:, columns].astype(jnp.float32)
        for ref in in_refs[1:]:
            total = total + ref[:, columns].astype(jnp.float32)
        for n, ref in enumerate(out_refs):
            ref[:, columns] = total[n * size : (n + 1) * size].astype(ref.dtype)


def fold(values, pieces):
    rows, width = values[0].shape
    return pl.pallas_call(
        functools.partial(fold_kernel, len(values)),
        in_specs=whole_vmem(len(values)),
        out_specs=whole_vmem(pieces),
        out_shape=[VMEM((rows // pieces, width), values[0].dtype)] * pieces,
        compiler_params=limit(1024 * 1024 + 12 * rows * FOLD_BLOCK),
    )(*[in_vmem(v) for v in values])


def line_steps(lines):
    steps = []
    while lines > 1:
        radix = min(4, lines)
        lines //= radix
        near, wide = 2 * lines, 4 * lines
        if radix == 4:
            out = [(wide, near), (near, wide), (near + wide, near + wide)]
            steps.append((out, [(near, wide), (wide, near)]))
        else:
            steps.append(([(near, near)], [(near, near)]))
    return steps


def give_back(own, far, groups, members):
    values = [own, swap(far, "expert", members, 1)]
    for masks in [(2, 1), (1, 2)]:
        keep, send = fold(values, 2)
        values = [keep, swap_group(send, groups, members, masks)]
    for _, back in reversed(line_steps(members // 2)):
        for masks in back:
            keep, send = fold(values, 2)
            values = [keep, swap(send, "expert", members, masks)]
    total = values[0].astype(jnp.float32) + values[1].astype(jnp.float32)
    return total.astype(jnp.bfloat16)


def on_device(tokens, expert_ids, gate_weights, w_gate, w_up, w_down):
    groups = lax.axis_size("group")
    members = lax.axis_size("expert")
    split = members // EXP_GRP
    me = lax.axis_index("group") * EXP_GRP + lax.axis_index("expert") // split
    me = me.astype(jnp.int32).reshape(1)
    blocks = w_gate.shape[2] // UNIT_BLOCK
    gates, ups = max(1, blocks * 5 // 8), max(1, blocks // 2)
    gate_cuts = [0, max(1, gates * 3 // 5), gates, gates]
    up_cuts = [0, 0, ups // 4, ups]
    jobs, place, count = [], {}, 0
    for n in range(3):
        pieces = [
            (m, list(range(cuts[n], cuts[n + 1]))) for m, cuts in enumerate([gate_cuts, up_cuts])
        ]
        job = []
        for m, inside in pieces:
            if inside:
                job.append(((w_gate, w_up)[m], inside[0] * UNIT_BLOCK, len(inside) * UNIT_BLOCK))
                for i, b in enumerate(inside):
                    place[m, b] = (count, i * UNIT_BLOCK)
                count += 1
        jobs.append(job)
    order = list(range(min(2, ups)))
    fixed, loose = list(range(len(order), gates)), list(range(gates, blocks))
    while fixed or loose:
        order += loose[:1] + fixed[:1]
        fixed, loose = fixed[1:], loose[1:]

    value = pack(me, tokens, expert_ids, gate_weights)
    width = tokens.shape[1] // 2
    halves = [(0, width), (width, width + LANES)]
    held, mark = fetch(jobs[0], value)
    for masks, _ in line_steps(members // 2):
        line = [value] + [swap(value, "expert", members, m) for m in masks]
        (value,) = join(line, mark)
    got = swap_group(value, groups, members, (1, 2))
    more, mark = fetch(jobs[1], value)
    held += more
    a, b = join([value, got], mark, halves)
    a_got, b_got = [swap_group(v, groups, members, (2, 1)) for v in (a, b)]
    a_core, b_core = swap(a, "expert", members, 1), swap(b, "expert", members, 1)
    more, mark = fetch(jobs[2], a)
    held += more
    (a_got,), (b_got,) = hold([a_got], mark), hold([b_got], mark)
    a_parts = [a, a_got, a_core, swap(a_got, "expert", members, 1)]
    b_parts = [b, b_got, b_core, swap(b_got, "expert", members, 1)]
    sums = run_expert(a_parts, b_parts, held, place, order, w_gate, w_up, w_down, me)
    out = [give_back(own, far, groups, members) for own, far in zip(sums[:2], sums[2:])]
    return jnp.concatenate(out, axis=1)


def solution(mesh):
    in_specs = (
        P(AXES, None),
        P(AXES, None),
        P(AXES, None),
        P(AXES, None, None),
        P(AXES, None, None),
        P(AXES, None, None),
    )
    out_specs = P(AXES, None)
    return jax.shard_map(
        on_device, mesh=mesh, in_specs=in_specs, out_specs=out_specs, check_vma=False
    )
```

```python
import functools

import jax
import jax.numpy as jnp
from jax import lax
from jax.experimental import pallas as pl
from jax.experimental.pallas import tpu as pltpu
from jax.sharding import PartitionSpec as P

EXP_GRP = 8
LANES = 128
AXES = ("group", "expert")
VMEM = pltpu.VMEM
UNIT_BLOCK = 256
DOWN_BLOCK = 512
RING = 3
DOWN_RING = 5
FOLD_BLOCK = 1024


def in_vmem(value):
    return pltpu.with_memory_space_constraint(value, VMEM)


def in_hbm(value):
    return pltpu.with_memory_space_constraint(value, pltpu.HBM)


def whole_vmem(count):
    return [pl.BlockSpec(memory_space=VMEM)] * count


def swap(value, axis, size, mask):
    return lax.ppermute(value, axis, [(i, i ^ mask) for i in range(size)])


def swap_group(value, groups, members, masks):
    pairs = []
    for g in range(groups):
        for e in range(members):
            pairs.append((g * members + e, (g ^ masks[e % 2]) * members + e))
    return lax.ppermute(value, AXES, pairs)


def limit(amount):
    return pltpu.CompilerParams(vmem_limit_bytes=int(amount))


def cost(flops, amount):
    return pl.CostEstimate(flops=flops, bytes_accessed=amount, transcendentals=0)


def pack_kernel(me_ref, tokens_ref, ids_ref, weights_ref, out_ref):
    width = tokens_ref.shape[1]
    out_ref[:, :width] = tokens_ref[...]
    ids = ids_ref[...]
    weights = weights_ref[...].astype(jnp.float32)
    label = lax.broadcasted_iota(jnp.int32, (ids.shape[0], LANES), 1)
    route = jnp.zeros((ids.shape[0], LANES), jnp.float32)
    for k in range(ids.shape[1]):
        route += jnp.where(ids[:, k : k + 1] == label, weights[:, k : k + 1], 0.0)
    out_ref[:, width:] = route.astype(out_ref.dtype)


def pack(me, tokens, expert_ids, gate_weights):
    rows, width = tokens.shape
    args = (tokens, expert_ids, gate_weights)
    return pl.pallas_call(
        pack_kernel,
        grid=(1,),
        in_specs=[pl.BlockSpec(memory_space=pltpu.SMEM)]
        + [pl.BlockSpec(a.shape, lambda i: (0, 0)) for a in args],
        out_specs=whole_vmem(1)[0],
        out_shape=VMEM((rows, width + LANES), tokens.dtype),
        compiler_params=limit(2 * 1024 * 1024),
    )(me, *[in_hbm(a) for a in args])


def fetch_kernel(jobs, *refs):
    src_refs = refs[: len(jobs)]
    out_refs = refs[len(jobs) + 1 : 2 * len(jobs) + 1]
    mark_ref, sems = refs[-2:]
    copies = []
    for n, (_, first, columns) in enumerate(jobs):
        size = src_refs[n].shape[1] // 4
        for i in range(4):
            copies.append(
                pltpu.make_async_copy(
                    src_refs[n].at[0, pl.ds(i * size, size), pl.ds(first, columns)],
                    out_refs[n].at[pl.ds(i * size, size), :],
                    sems.at[n * 4 + i],
                )
            )
    for copy in copies:
        copy.start()
    mark_ref[...] = jnp.zeros_like(mark_ref)
    for copy in copies:
        copy.wait()


def fetch(jobs, after):
    if not jobs:
        return [], None
    rows = jobs[0][0].shape[1]
    hbm = pl.BlockSpec(memory_space=pltpu.HBM)
    *out, mark = pl.pallas_call(
        functools.partial(fetch_kernel, jobs),
        in_specs=[hbm] * len(jobs) + [pl.BlockSpec(memory_space=pl.ANY)],
        out_specs=whole_vmem(len(jobs) + 1),
        out_shape=[VMEM((rows, columns), w.dtype) for w, _, columns in jobs]
        + [VMEM((8, LANES), jnp.float32)],
        scratch_shapes=[pltpu.SemaphoreType.DMA((4 * len(jobs),))],
        compiler_params=limit(256 * 1024),
        cost_estimate=cost(0, sum(2 * rows * columns for _, _, columns in jobs)),
    )(*[in_hbm(w) for w, _, _ in jobs], after)
    return out, mark


def join_kernel(cuts, *refs):
    in_refs, out_refs = refs[: -len(cuts) - 1], refs[-len(cuts) :]
    for (start, size), out_ref in zip(cuts, out_refs):
        pieces = [r[:, start : start + size].astype(jnp.float32) for r in in_refs]
        out_ref[...] = jnp.concatenate(pieces, axis=0).astype(out_ref.dtype)


def join(values, after, cuts=None):
    rows = sum(v.shape[0] for v in values)
    width = values[0].shape[1]
    cuts = cuts or [(0, width)]
    after = values[0] if after is None else after
    return pl.pallas_call(
        functools.partial(join_kernel, cuts),
        in_specs=whole_vmem(len(values)) + [pl.BlockSpec(memory_space=pl.ANY)],
        out_specs=whole_vmem(len(cuts)),
        out_shape=[VMEM((rows, size), values[0].dtype) for _, size in cuts],
        compiler_params=limit(1024 * 1024 + 8 * rows * width),
    )(*[in_vmem(v) for v in values], after)


def hold_kernel(*refs):
    pass


def hold(values, after):
    if after is None:
        return values
    return pl.pallas_call(
        hold_kernel,
        in_specs=[pl.BlockSpec(memory_space=pl.ANY)] * (len(values) + 1),
        out_specs=[pl.BlockSpec(memory_space=pl.ANY)] * len(values),
        out_shape=[jax.ShapeDtypeStruct(v.shape, v.dtype) for v in values],
        input_output_aliases={i: i for i in range(len(values))},
        compiler_params=limit(256 * 1024),
    )(*values, after)


def times(left_ref, right_ref):
    return jnp.dot(left_ref[...], right_ref[...], preferred_element_type=jnp.float32)


def expert_kernel(place, order, streams, held, *refs):
    x_refs, w_refs, refs = refs[:8], refs[8 : 8 + held], refs[8 + held :]
    hbm, down_hbm, me_ref = refs[:2], refs[2], refs[3]
    own_refs, far_refs = refs[4:6], refs[6:8]
    x, hidden, scale_ref, ring, down_ring, sems, down_sem = refs[8:]
    depth, units = x.shape[1], hidden.shape[1]
    blocks = units // UNIT_BLOCK
    downs = depth // DOWN_BLOCK

    def copy(n):
        m, b = streams[n]
        return pltpu.make_async_copy(
            hbm[m].at[0, :, pl.ds(b * UNIT_BLOCK, UNIT_BLOCK)], ring.at[n % RING], sems.at[n % RING]
        )

    def down_copy(d, slot):
        return pltpu.make_async_copy(
            down_hbm.at[0, :, pl.ds(d * DOWN_BLOCK, DOWN_BLOCK)],
            down_ring.at[slot],
            down_sem.at[slot],
        )

    later = {}
    for n in range(min(DOWN_RING, downs)):
        later.setdefault(min(blocks - 1, 3 + n), []).append(down_copy(n, n))
    for n in range(min(RING, len(streams))):
        copy(n).start()

    part = x_refs[0].shape[0]
    width = depth // 2
    for n in range(4):
        rows = slice(n * part, (n + 1) * part)
        x[rows, :width] = x_refs[n][...]
        x[rows, width:] = x_refs[4 + n][:, :width]
        route = x_refs[4 + n][:, width:].astype(jnp.float32)
        lane = lax.broadcasted_iota(jnp.int32, route.shape, 1)
        scale = jnp.sum(jnp.where(lane == me_ref[0], route, 0.0), axis=1, keepdims=True)
        scale_ref[rows, :] = jnp.broadcast_to(scale, route.shape)

    def finish(b, gate, up):
        hidden[:, b * UNIT_BLOCK : (b + 1) * UNIT_BLOCK] = (jax.nn.silu(gate) * up).astype(
            jnp.bfloat16
        )

    waiting = None
    for turn, b in enumerate(order):
        weights, used = [], []
        for m in range(2):
            if (m, b) in place:
                where, first = place[m, b]
                weights.append(w_refs[where].at[:, first : first + UNIT_BLOCK])
            else:
                n = streams.index((m, b))
                copy(n).wait()
                weights.append(ring.at[n % RING])
                used.append(n)
        gate, up = [times(x, w) for w in weights]
        if waiting:
            finish(*waiting)
        waiting = (b, gate, up)
        for n in used:
            if n + RING < len(streams):
                copy(n + RING).start()
        for piece in later.get(turn, []):
            piece.start()
    finish(*waiting)

    for first in range(0, downs, 2):
        pair = range(first, min(first + 2, downs))
        for d in pair:
            down_copy(d, d % DOWN_RING).wait()
        for d in pair:
            value = times(hidden, down_ring.at[d % DOWN_RING]) * scale_ref[:, :1]
            value = value.astype(jnp.bfloat16)
            half, at = divmod(d * DOWN_BLOCK, width)
            own_refs[half][:, at : at + DOWN_BLOCK] = value[: 2 * part]
            far_refs[half][:, at : at + DOWN_BLOCK] = value[2 * part :]
        for d in pair:
            if d + DOWN_RING < downs:
                down_copy(d + DOWN_RING, d % DOWN_RING).start()


def run_expert(a_parts, b_parts, held, place, order, w_gate, w_up, w_down, me):
    rows = sum(p.shape[0] for p in a_parts)
    depth, units = w_up.shape[1], w_up.shape[2]
    half = VMEM((rows // 2, depth // 2), jnp.bfloat16)
    hbm = pl.BlockSpec(memory_space=pltpu.HBM)
    streams = [(m, b) for b in order for m in range(2) if (m, b) not in place]
    ring = max(1, min(RING, len(streams)))
    scratch = 2 * (
        rows * (depth + units + 2 * LANES)
        + ring * depth * UNIT_BLOCK
        + DOWN_RING * units * DOWN_BLOCK
    )
    work = 1024 * 1024 + 12 * rows * UNIT_BLOCK + 4 * rows * DOWN_BLOCK
    args = [in_vmem(v) for v in [*a_parts, *b_parts, *held]]
    return pl.pallas_call(
        functools.partial(expert_kernel, place, order, streams, len(held)),
        in_specs=whole_vmem(len(args)) + [hbm] * 3 + [pl.BlockSpec(memory_space=pltpu.SMEM)],
        out_specs=whole_vmem(4),
        out_shape=(half,) * 4,
        scratch_shapes=[
            VMEM((rows, depth), jnp.bfloat16),
            VMEM((rows, units), jnp.bfloat16),
            VMEM((rows, LANES), jnp.float32),
            VMEM((ring, depth, UNIT_BLOCK), jnp.bfloat16),
            VMEM((DOWN_RING, units, DOWN_BLOCK), jnp.bfloat16),
            pltpu.SemaphoreType.DMA((ring,)),
            pltpu.SemaphoreType.DMA((DOWN_RING,)),
        ],
        compiler_params=limit(scratch + work),
        cost_estimate=cost(6 * rows * depth * units, 4 * depth * units),
    )(*args, in_hbm(w_gate), in_hbm(w_up), in_hbm(w_down), me)


def fold_kernel(count, *refs):
    in_refs, out_refs = refs[:count], refs[count:]
    size = out_refs[0].shape[0]
    for first in range(0, in_refs[0].shape[1], FOLD_BLOCK):
        columns = slice(first, first + FOLD_BLOCK)
        total = in_refs[0][:, columns].astype(jnp.float32)
        for ref in in_refs[1:]:
            total = total + ref[:, columns].astype(jnp.float32)
        for n, ref in enumerate(out_refs):
            ref[:, columns] = total[n * size : (n + 1) * size].astype(ref.dtype)


def fold(values, pieces):
    rows, width = values[0].shape
    return pl.pallas_call(
        functools.partial(fold_kernel, len(values)),
        in_specs=whole_vmem(len(values)),
        out_specs=whole_vmem(pieces),
        out_shape=[VMEM((rows // pieces, width), values[0].dtype)] * pieces,
        compiler_params=limit(1024 * 1024 + 12 * rows * FOLD_BLOCK),
    )(*[in_vmem(v) for v in values])


def line_steps(lines):
    steps = []
    while lines > 1:
        radix = min(4, lines)
        lines //= radix
        near, wide = 2 * lines, 4 * lines
        if radix == 4:
            steps.append(([near, wide, near + wide], [wide, near]))
        else:
            steps.append(([near], [near]))
    return steps


def give_back(own, far, groups, members):
    values = [own, swap(far, "expert", members, 1)]
    for masks in [(2, 1), (1, 2)]:
        keep, send = fold(values, 2)
        values = [keep, swap_group(send, groups, members, masks)]
    for _, back in reversed(line_steps(members // 2)):
        for mask in back:
            keep, send = fold(values, 2)
            values = [keep, swap(send, "expert", members, mask)]
    total = values[0].astype(jnp.float32) + values[1].astype(jnp.float32)
    return total.astype(jnp.bfloat16)


def on_device(tokens, expert_ids, gate_weights, w_gate, w_up, w_down):
    groups = lax.axis_size("group")
    members = lax.axis_size("expert")
    split = members // EXP_GRP
    me = lax.axis_index("group") * EXP_GRP + lax.axis_index("expert") // split
    me = me.astype(jnp.int32).reshape(1)
    blocks = w_gate.shape[2] // UNIT_BLOCK
    gates, ups = max(1, blocks * 5 // 8), max(1, blocks // 2)
    gate_cuts = [0, max(1, gates * 3 // 5), gates, gates]
    up_cuts = [0, 0, ups // 4, ups]
    jobs, place, count = [], {}, 0
    for n in range(3):
        pieces = [
            (m, list(range(cuts[n], cuts[n + 1]))) for m, cuts in enumerate([gate_cuts, up_cuts])
        ]
        job = []
        for m, inside in pieces:
            if inside:
                job.append(((w_gate, w_up)[m], inside[0] * UNIT_BLOCK, len(inside) * UNIT_BLOCK))
                for i, b in enumerate(inside):
                    place[m, b] = (count, i * UNIT_BLOCK)
                count += 1
        jobs.append(job)
    order = list(range(min(2, ups)))
    fixed, loose = list(range(len(order), gates)), list(range(gates, blocks))
    while fixed or loose:
        order += loose[:1] + fixed[:1]
        fixed, loose = fixed[1:], loose[1:]

    value = pack(me, tokens, expert_ids, gate_weights)
    width = tokens.shape[1] // 2
    halves = [(0, width), (width, width + LANES)]
    held, mark = fetch(jobs[0], value)
    for masks, _ in line_steps(members // 2):
        line = [value] + [swap(value, "expert", members, m) for m in masks]
        (value,) = join(line, mark)
    got = swap_group(value, groups, members, (1, 2))
    more, mark = fetch(jobs[1], value)
    held += more
    a, b = join([value, got], mark, halves)
    a_got, b_got = [swap_group(v, groups, members, (2, 1)) for v in (a, b)]
    more, mark = fetch(jobs[2], a)
    held += more
    (a_got,), (b_got,) = hold([a_got], mark), hold([b_got], mark)
    (a_late,), (b_late,) = join([a], mark), join([b], mark)
    a_parts = [a, a_got] + [swap(v, "expert", members, 1) for v in (a_late, a_got)]
    b_parts = [b, b_got] + [swap(v, "expert", members, 1) for v in (b_late, b_got)]
    sums = run_expert(a_parts, b_parts, held, place, order, w_gate, w_up, w_down, me)
    out = [give_back(own, far, groups, members) for own, far in zip(sums[:2], sums[2:])]
    return jnp.concatenate(out, axis=1)


def solution(mesh):
    in_specs = (
        P(AXES, None),
        P(AXES, None),
        P(AXES, None),
        P(AXES, None, None),
        P(AXES, None, None),
        P(AXES, None, None),
    )
    out_specs = P(AXES, None)
    return jax.shard_map(
        on_device, mesh=mesh, in_specs=in_specs, out_specs=out_specs, check_vma=False
    )
```
